256 devices in a mesh: vox: 8 (over x, core), mem: 32 (over y, z).
Axes of the slice: x: 4, y: 4, z: 8, core: 2. Of those that a mesh axis runs over, the one named last changes fastest.
Arguments:
- ensemble: bfloat16 [256, 524288], P('mem', 'vox'), may hold values from -6 to 6
- partials: float32 [8, 256, 131072], P('vox', 'mem'), may hold values from -6 to 6
- perturb: float32 [256, 131072], P('mem', 'vox'), may hold values from -6 to 6
- observed: float32 [131072], P('vox'), may hold values from -6 to 6
- variance: float32 [131072], P('vox'), may hold values from 0.5 to 2
- obs_lists: int32 [4096, 64], P(('vox', 'mem')), may hold values from 0 to 127, all different within a row
- taper_index: int32 [4096, 64], P(('vox', 'mem')), may hold values from 0 to 15
- taper_table: float32 [16], replicated, may hold values from 0.1 to 1
Outputs:
- updated: bfloat16 [256, 524288], P('mem', 'vox')
The draws below stay inside these ranges and needn't reach their ends.
All inputs are finite; a program needn't handle non-finite values.
Results may differ from the reference program's by a relative error of at most 0.017.
Values may be sent and summed in bfloat16 or wider, within the bound.
A program may use at most 128 MiB of HBM per device.

```python
import math
import jax
import jax.numpy as jnp
from jax import lax

K = 256
BS = 128
OB = 128
NT = 16
OBG = 128
L = 64
NOBS = 131072
NBLK = 4096
NCELL = 524288
N_VOX = 8


def place_ends(values, stream_key, low, largest):
    extent = values.shape
    place = [jax.random.randint(jax.random.fold_in(stream_key, axis), (), 0, extent[axis]) for axis in range(len(extent))]
    values = values.at[tuple(place)].set(low)
    longest = extent.index(max(extent))
    place[longest] = (place[longest] + 1) % extent[longest]
    return values.at[tuple(place)].set(largest)


def spiked(drawn, stream_key, source, target, blocks, factor):
    owner, partner = [(jnp.arange(drawn.shape[position]) // (drawn.shape[position] // blocks)).reshape([-1 if axis == position else 1 for axis in range(drawn.ndim)]) for position in (source, target)]
    chosen = jax.random.permutation(stream_key, blocks)[partner]
    strong = (owner == chosen) | (owner == (partner + blocks // 2) % blocks)
    return jnp.where(strong, factor * drawn, drawn)


def levels(own_key, shape, cuts, low, largest):
    gain, own = 1.0, jax.random.fold_in(own_key, 6)
    for dim, blocks in cuts:
        draws = jnp.exp(jax.random.uniform(jax.random.fold_in(own, dim), (blocks,), jnp.float32, low / len(cuts), largest / len(cuts)))
        gain = gain * jnp.repeat(draws, shape[dim] // blocks).reshape([-1 if axis == dim else 1 for axis in range(len(shape))])
    return gain


def distinct(rng, rows, amount, top, lift):
    order = jax.random.permutation(jax.random.fold_in(rng, 1), amount)
    boost = order
    for power in range(3):
        boost = boost * boost // amount
    boost = boost * lift // amount
    chance = jax.random.randint(jax.random.fold_in(rng, 2), (rows, amount), 0, 4096) + boost
    holders = jax.random.permutation(jax.random.fold_in(rng, 3), rows)[jnp.arange(amount) % rows]
    chance = jnp.where(jnp.arange(rows)[:, None] == holders[None, :], 1 << 14, chance)
    priority = chance * amount + jnp.arange(amount)
    return lax.top_k(priority.astype(jnp.int32), top)[1].astype(jnp.int32)


def centred(own_key, dims, spread, limit, split=(), held_as=jnp.bfloat16):
    gain = levels(own_key, dims, split, -0.22, 0.18) if split else 1.0
    values = jax.random.normal(own_key, dims, jnp.float32) * spread * gain
    return jnp.minimum(jnp.maximum(values, -limit), limit).astype(held_as)


def bell_draw_with(stream_key, shape, deviation, limit, cuts, heavy, kind=jnp.bfloat16):
    values = deviation * jax.random.normal(stream_key, shape, jnp.float32)
    if cuts:
        values = values * levels(stream_key, shape, cuts, -0.22, 0.18)
    return jnp.clip(spiked(values, jax.random.fold_in(stream_key, 3), *heavy), -limit, limit).astype(kind)


def setup_inputs(seed: int = 0) -> dict:
    arg_keys = jax.random.split(jax.random.key(seed), 9)
    ensemble = centred(arg_keys[0], (K, NCELL), 1.0, 6.0, ((0, 32), (1, 8)))
    partials = bell_draw_with(arg_keys[1], (N_VOX, K, NOBS), 0.35, 6.0, ((0, 8), (1, 32)), (0, 2, 8, 2.0), jnp.float32)
    perturb = centred(arg_keys[2], (K, NOBS), 0.5, 6.0, ((0, 32), (1, 8)), jnp.float32)
    observed = centred(arg_keys[3], (NOBS,), 1.0, 6.0, ((0, 8),), jnp.float32)
    variance = jnp.clip(jnp.exp(math.log(2.0) - 1.3862944 * jax.random.uniform(arg_keys[4], (NOBS,), jnp.float32) ** levels(arg_keys[4], (NOBS,), ((0, 8),), -0.2, 0.2)), 0.5, 2.0)
    obs_lists = distinct(arg_keys[5], NBLK, OBG, L, 0)
    taper_index = place_ends(jax.random.randint(arg_keys[6], (NBLK, L), 0, NT), jax.random.fold_in(arg_keys[6], 1), 0, NT - 1).astype(jnp.int32)
    taper_table = jnp.clip(jax.random.uniform(arg_keys[7], (NT,), jnp.float32, 0.1, 1.0), 0.1, 1.0)
    return dict(ensemble=ensemble, partials=partials, perturb=perturb, observed=observed, variance=variance, obs_lists=obs_lists, taper_index=taper_index, taper_table=taper_table)


def reference(ensemble, partials, perturb, observed, variance, obs_lists, taper_index, taper_table):
    high = lax.Precision.HIGHEST
    predicted = jnp.sum(partials, axis=0).astype(jnp.bfloat16)
    pred_f = predicted.astype(jnp.float32)
    weights = ((observed[None, :] + perturb - pred_f) / variance[None, :]).astype(jnp.bfloat16)
    obs_anom = (pred_f - jnp.mean(pred_f, axis=0, keepdims=True)).astype(jnp.bfloat16)
    state_f = ensemble.astype(jnp.float32)
    state_anom = (state_f - jnp.mean(state_f, axis=0, keepdims=True)).astype(jnp.bfloat16)
    tapers = taper_table[taper_index]
    picks = (obs_lists[:, :, None] == jnp.arange(OBG, dtype=jnp.int32)[None, None, :]).astype(jnp.float32)
    coeff = jnp.sum(tapers[:, :, None] * picks, axis=1)
    group_obs = OBG * OB
    group_blocks = NBLK // N_VOX

    def one_group(g):
        start = (g * group_obs).astype(jnp.int32)
        yc = lax.dynamic_slice_in_dim(obs_anom, start, group_obs, 1).reshape(K, OBG, OB).astype(jnp.float32)
        wt = lax.dynamic_slice_in_dim(weights, start, group_obs, 1).reshape(K, OBG, OB).astype(jnp.float32)
        moments = jnp.einsum("kbi,lbi->bkl", yc, wt, precision=high)
        cg = lax.dynamic_slice_in_dim(coeff, (g * group_blocks).astype(jnp.int32), group_blocks, 0)
        combined = jnp.einsum("bo,okl->bkl", cg, moments, precision=high).astype(jnp.bfloat16)
        cstart = (g * group_blocks * BS).astype(jnp.int32)
        xa = lax.dynamic_slice_in_dim(state_anom, cstart, group_blocks * BS, 1).reshape(K, group_blocks, BS).astype(jnp.float32)
        xo = lax.dynamic_slice_in_dim(state_f, cstart, group_blocks * BS, 1)
        increment = jnp.einsum("kbc,bkl->lbc", xa, combined.astype(jnp.float32), precision=high).reshape(K, group_blocks * BS)
        return (xo + increment * (1.0 / (K - 1))).astype(jnp.bfloat16)

    result = lax.map(one_group, jnp.arange(N_VOX, dtype=jnp.int32))
    return jnp.transpose(result, (1, 0, 2)).reshape(K, NCELL)
```

```python
import functools

import jax
import jax.numpy as jnp
from jax import lax
from jax.experimental import pallas as pl
from jax.experimental.pallas import tpu as pltpu
from jax.sharding import PartitionSpec as P

MESH = pl.DeviceIdType.MESH
NX, NC, NY, NZ = 4, 2, 4, 8
NS = NX * NC
MEM = 8
BLK = 128
F32, BF16 = jnp.float32, jnp.bfloat16


def kernel(
    ens, par, per, obs, var, coef, out,
    par_v, per_v, obs_v, core_send, core_recv, rs_send, rs_recv, own_sum,
    a0, a1, a2, vh, ch, p1, p_all, x1, x_all, wt, m_f, m_all, comb, ost,
    ld_s, loc_s,
    co_ss, co_rs, rs_ss, rs_rs, x1_ss, x1_rs, a1_ss, a1_rs, v_ss, v_rs, c_ss, c_rs,
    xz_ss, xz_rs, az_ss, az_rs, pz_ss, pz_rs, py_ss, py_rs, xy_ss, xy_rs,
    mx_ss, mx_rs, mc_ss, mc_rs, o_ss, o_rs,
):
    v = lax.axis_index("vox")
    mem = lax.axis_index("mem")
    x, c = v // NC, lax.rem(v, NC)
    y, z = mem // NZ, lax.rem(mem, NZ)
    oc = 1 - c
    cells = ens.shape[1] // NS
    data = per.shape[1] // NS
    nob = data // BLK
    nvb = cells // BLK
    nl = NZ * MEM

    def dev(vox, yy, zz):
        return (vox, yy * NZ + zz)

    def rc(src, dst, ss, rs, to):
        return pltpu.make_async_remote_copy(
            src_ref=src, dst_ref=dst, send_sem=ss, recv_sem=rs, device_id=to, device_id_type=MESH
        )

    def mod(a, n):
        return lax.rem(a, n)

    loads = [
        pltpu.make_async_copy(par.at[0], par_v, ld_s.at[0]),
        pltpu.make_async_copy(per, per_v, ld_s.at[1]),
        pltpu.make_async_copy(obs, obs_v, ld_s.at[2]),
    ]
    for cp in loads:
        cp.start()

    barrier = pltpu.get_barrier_semaphore()

    def greet(to):
        pl.semaphore_signal(barrier, inc=1, device_id=to, device_id_type=MESH)

    for d in range(1, NS):
        greet(dev(mod(v + d, NS), y, z))
        greet(dev(v, y, mod(z + d, NZ)))
    for d in range(1, NY):
        greet(dev(v, mod(y + d, NY), z))
    home_diag = v == z
    c_to = mem // 4
    c_row = lax.rem(mem, 4)
    for j in range(4):
        src_mem = 4 * v + j
        is_self = jnp.logical_and(home_diag, src_mem == mem)

        @pl.when(jnp.logical_not(is_self))
        def _():
            greet((z, src_mem))

    for s in range(NS):
        is_self = jnp.logical_and(home_diag, v == s)

        @pl.when(jnp.logical_not(is_self))
        def _():
            greet(dev(s, y, v))

    c_self = jnp.logical_and(home_diag, c_to == v)

    loads[0].wait()

    def cast_one(i, carry):
        xx, g = i // NZ, lax.rem(i, NZ)
        col = pl.multiple_of(g * (NS * data) + (NC * xx + oc) * data, data)
        core_send[xx, g] = par_v[:, pl.ds(col, data)].astype(BF16)
        return carry

    lax.fori_loop(0, NX * NZ, cast_one, 0)
    loads[1].wait()
    loads[2].wait()
    for s in range(NS):
        a0[s] = (per_v[:, s * data:(s + 1) * data] + obs_v[:, s * data:(s + 1) * data]).astype(BF16)

    pl.semaphore_wait(
        barrier,
        (NS - 1) + (NZ - 1) + (NY - 1)
        + 4 - c_self.astype(jnp.int32)
        + NZ - home_diag.astype(jnp.int32),
    )

    sends = []

    def start(cp):
        cp.start()
        sends.append(cp)

    partner = dev(NC * x + oc, y, z)
    for e in (1, 3, 2, 0):
        xx = mod(x + e, NX)
        start(rc(core_send.at[xx], core_recv.at[xx], co_ss.at[e], co_rs.at[xx], partner))

    own_x = pltpu.make_async_copy(ens.at[:, pl.ds(pl.multiple_of(v * cells, cells), cells)], x1.at[v], x1_rs.at[v])
    own_x.start()
    own_a = pltpu.make_async_copy(a0.at[v], a1.at[v], a1_rs.at[v])
    own_a.start()
    for d in range(1, NS):
        to = mod(v + d, NS)
        start(rc(a0.at[to], a1.at[v], a1_ss.at[d], a1_rs.at[v], dev(to, y, z)))
        start(rc(ens.at[:, pl.ds(pl.multiple_of(to * cells, cells), cells)], x1.at[v], x1_ss.at[d], x1_rs.at[v], dev(to, y, z)))

    @pl.when(home_diag)
    def _():
        pltpu.make_async_copy(var.at[v], vh, v_rs).start()
        for d in range(1, NS):
            to = mod(v + d, NS)
            rc(var.at[to], vh, v_ss.at[d], v_rs, dev(to, y, z)).start()

    for yy in range(NY):
        is_self = jnp.logical_and(c_self, y == yy)

        @pl.when(is_self)
        def _():
            pltpu.make_async_copy(coef, ch.at[c_row], c_rs.at[c_row]).start()

        @pl.when(jnp.logical_not(is_self))
        def _():
            rc(coef, ch.at[c_row], c_ss.at[yy], c_rs.at[c_row], dev(c_to, yy, v)).start()

    for e in (1, 3, 2, 0):
        xx = mod(x + e, NX)
        rc(core_send.at[xx], core_recv.at[xx], co_ss.at[e], co_rs.at[xx], partner).wait_recv()

        def sum_one(g, carry):
            col = pl.multiple_of(g * (NS * data) + (NC * xx + c) * data, data)
            total = par_v[:, pl.ds(col, data)] + core_recv[xx, g].astype(F32)
            if e == 0:
                own_sum[g] = total
            else:
                rs_send[e - 1, g] = total.astype(BF16)
            return carry

        lax.fori_loop(0, NZ, sum_one, 0)
        if e:
            start(rc(rs_send.at[e - 1], rs_recv.at[e - 1], rs_ss.at[e - 1], rs_rs.at[e - 1], dev(NC * xx + c, y, z)))

    for d in range(NZ):
        g = mod(z + d, NZ)
        pltpu.make_async_copy(x1.at[g], x1.at[g], x1_rs.at[g]).wait()
        pltpu.make_async_copy(a1.at[g], a1.at[g], a1_rs.at[g]).wait()
        if d == 0:
            pltpu.make_async_copy(x1.at[g], x_all.at[y, z], xz_rs.at[z]).start()
            pltpu.make_async_copy(a1.at[g], a2.at[z], az_rs.at[z]).start()
        else:
            start(rc(a1.at[g], a2.at[z], az_ss.at[d], az_rs.at[z], dev(v, y, g)))
            start(rc(x1.at[g], x_all.at[y, z], xz_ss.at[d], xz_rs.at[z], dev(v, y, g)))

    for e in range(1, NX):
        rc(rs_send.at[e - 1], rs_recv.at[e - 1], rs_ss.at[e - 1], rs_rs.at[e - 1], partner).wait_recv()

    def pred_one(g, carry):
        total = own_sum[g]
        for e in range(NX - 1):
            total += rs_recv[e, g].astype(F32)
        p1[g] = total.astype(BF16)
        return carry

    lax.fori_loop(0, NZ, pred_one, 0)
    pltpu.make_async_copy(p1.at[z], p_all.at[y, z], pz_rs.at[z]).start()
    for d in range(1, NZ):
        g = mod(z + d, NZ)
        start(rc(p1.at[g], p_all.at[y, z], pz_ss.at[d], pz_rs.at[z], dev(v, y, g)))

    def spread_x(e):
        zs = mod(z + NZ - e, NZ)
        pltpu.make_async_copy(x_all.at[y, zs], x_all.at[y, zs], xz_rs.at[zs]).wait()
        for d in range(1, NY):
            start(rc(x_all.at[y, zs], x_all.at[y, zs], xy_ss.at[d, e], xy_rs.at[y, zs], dev(v, mod(y + d, NY), z)))

    for e in range(4):
        spread_x(e)

    for e in range(NZ):
        zs = mod(z + NZ - e, NZ)
        pltpu.make_async_copy(p_all.at[y, zs], p_all.at[y, zs], pz_rs.at[zs]).wait()
    for d in range(1, NY):
        start(rc(p_all.at[y], p_all.at[y], py_ss.at[d], py_rs.at[y], dev(v, mod(y + d, NY), z)))

    for e in range(4, NZ):
        spread_x(e)

    for e in range(NZ):
        zs = mod(z + NZ - e, NZ)
        pltpu.make_async_copy(a2.at[zs], a2.at[zs], az_rs.at[zs]).wait()
    pltpu.make_async_copy(var.at[0], vh, v_rs).wait()

    def weight_one(o, carry):
        col = pl.ds(pl.multiple_of(o * BLK, BLK), BLK)
        innov = a2[:, :, col].astype(F32) - p_all[y, :, :, col].astype(F32)
        w = innov.reshape(nl, BLK) / vh[pl.ds(o, 1), :]
        wt[o] = w.astype(BF16)
        return carry

    lax.fori_loop(0, nob, weight_one, 0)

    for d in range(1, NY):
        ys = mod(y + d, NY)
        pltpu.make_async_copy(p_all.at[ys], p_all.at[ys], py_rs.at[ys]).wait()

    def moment_one(o, carry):
        col = pl.ds(pl.multiple_of(o * BLK, BLK), BLK)
        pred = p_all[:, :, :, col].astype(F32).reshape(NY * nl, BLK)
        anom = (pred - jnp.mean(pred, axis=0, keepdims=True)).astype(BF16)
        mom = lax.dot_general(wt[o], anom, (((1,), (1,)), ((), ())), preferred_element_type=F32)
        for h in range(2):
            m_f[h, pl.ds(o, nl, stride=nob), :] = mom[:, h * 128:(h + 1) * 128]
        return carry

    lax.fori_loop(0, nob, moment_one, 0)

    half = nl // 2
    for q in range(2):
        def cast_m(i, carry):
            rows = pl.ds(pl.multiple_of((q * half + i) * nob, nob), nob)
            for h in range(2):
                m_all[q, v, i, :, h * 128:(h + 1) * 128] = m_f[h, rows, :].astype(BF16)
            return carry

        lax.fori_loop(0, half, cast_m, 0)
        for e in range(1, NX):
            start(rc(m_all.at[q, v], m_all.at[q, v], mx_ss.at[q, e], mx_rs.at[q, v], dev(mod(v + NC * e, NS), y, z)))
        start(rc(m_all.at[q, v], m_all.at[q, v], mc_ss.at[q, 0], mc_rs.at[q, v], partner))

    for j in range(4):
        pltpu.make_async_copy(ch.at[j], ch.at[j], c_rs.at[j]).wait()
    coeff = ch[...].reshape(nvb, BLK)

    for q in range(2):
        for e in (1, 3, 2):
            vs = mod(v + NC * e, NS)
            pltpu.make_async_copy(m_all.at[q, vs], m_all.at[q, vs], mx_rs.at[q, vs]).wait()
            start(rc(m_all.at[q, vs], m_all.at[q, vs], mc_ss.at[q, e], mc_rs.at[q, vs], partner))
        for e in range(NX):
            vs = NC * mod(x + e, NX) + oc
            pltpu.make_async_copy(m_all.at[q, vs], m_all.at[q, vs], mc_rs.at[q, vs]).wait()

        def combine_one(i, carry):
            mom = m_all[q, :, i].reshape(NS * nob, NY * nl)
            com = jnp.dot(coeff, mom, preferred_element_type=F32)
            for h in range(2):
                comb[h, pl.ds(q * half + i, nvb, stride=nl), :] = com[:, h * 128:(h + 1) * 128]
            return carry

        lax.fori_loop(0, half, combine_one, 0)

    for d in range(1, NY):
        ys = mod(y + d, NY)
        for e in range(NZ):
            pltpu.make_async_copy(x_all.at[ys, e], x_all.at[ys, e], xy_rs.at[ys, e]).wait()

    parts = 4
    per_part = nvb // parts
    width = per_part * BLK
    for q in range(parts):
        def update_one(i, carry):
            b = q * per_part + i
            col = pl.ds(pl.multiple_of(b * BLK, BLK), BLK)
            state = x_all[:, :, :, col].astype(F32).reshape(NY * nl, BLK)
            anom = (state - jnp.mean(state, axis=0, keepdims=True)).astype(BF16)
            rows = pl.ds(pl.multiple_of(b * nl, nl), nl)
            inc = jnp.zeros((nl, BLK), F32)
            for h in range(2):
                inc += jnp.dot(
                    comb[h, rows, :].astype(BF16), anom[h * 128:(h + 1) * 128], preferred_element_type=F32
                )
            own = x_all[y, :, :, col].astype(F32)
            ost[:, :, col] = (own + inc.reshape(NZ, MEM, BLK) * (1.0 / (NY * nl - 1))).astype(BF16)
            return carry

        lax.fori_loop(0, per_part, update_one, 0)
        src_col = pl.ds(q * width, width)
        dst_col = pl.ds(pl.multiple_of(v * cells + q * width, width), width)
        for d in range(NZ):
            zt = mod(z + d, NZ)
            if d == 0:
                @pl.when(home_diag)
                def _():
                    pltpu.make_async_copy(ost.at[zt, :, src_col], out.at[:, dst_col], o_rs.at[q, v]).start()

                @pl.when(jnp.logical_not(home_diag))
                def _():
                    rc(ost.at[zt, :, src_col], out.at[:, dst_col], o_ss.at[q, 0], o_rs.at[q, v], dev(z, y, zt)).start()
            else:
                start(rc(ost.at[zt, :, src_col], out.at[:, dst_col], o_ss.at[q, d], o_rs.at[q, v], dev(z, y, zt)))

    for cp in sends:
        cp.wait_send()

    @pl.when(home_diag)
    def _():
        for d in range(1, NS):
            rc(var.at[0], vh, v_ss.at[d], v_rs, partner).wait_send()

    for yy in range(NY):
        @pl.when(jnp.logical_not(jnp.logical_and(c_self, y == yy)))
        def _():
            rc(coef, ch.at[c_row], c_ss.at[yy], c_rs.at[c_row], partner).wait_send()

    @pl.when(jnp.logical_not(home_diag))
    def _():
        for q in range(parts):
            rc(ost.at[0, :, pl.ds(0, width)], out.at[:, pl.ds(0, width)], o_ss.at[q, 0], o_rs.at[q, v], partner).wait_send()

    for q in range(parts):
        for s in range(NS):
            dst_col = pl.ds(s * cells + q * width, width)
            pltpu.make_async_copy(out.at[:, dst_col], out.at[:, dst_col], o_rs.at[q, s]).wait()


def local(ensemble, partials, perturb, observed, variance, obs_lists, taper_index, taper_table):
    groups = observed.shape[0] // BLK
    table_hits = (
        taper_index[:, :, None] == jnp.arange(taper_table.shape[0], dtype=jnp.int32)[None, None, :]
    ).astype(F32)
    tapers = jnp.sum(table_hits * taper_table[None, None, :], axis=2)
    picks = (obs_lists[:, :, None] == jnp.arange(groups, dtype=jnp.int32)[None, None, :]).astype(F32)
    coeff = jnp.sum(tapers[:, :, None] * picks, axis=1).astype(BF16)
    cells = ensemble.shape[1] // NS
    data = perturb.shape[1] // NS
    nob = data // BLK
    nl = NZ * MEM
    nvb = cells // BLK
    dma = pltpu.SemaphoreType.DMA
    return pl.pallas_call(
        kernel,
        out_shape=jax.ShapeDtypeStruct(ensemble.shape, BF16),
        in_specs=[pl.BlockSpec(memory_space=pl.ANY)] * 6,
        out_specs=pl.BlockSpec(memory_space=pl.ANY),
        scratch_shapes=[
            pltpu.VMEM(partials.shape[1:], F32),
            pltpu.VMEM(perturb.shape, F32),
            pltpu.VMEM((1, observed.shape[0]), F32),
            pltpu.VMEM((NX, NZ, MEM, data), BF16),
            pltpu.VMEM((NX, NZ, MEM, data), BF16),
            pltpu.VMEM((NX - 1, NZ, MEM, data), BF16),
            pltpu.VMEM((NX - 1, NZ, MEM, data), BF16),
            pltpu.VMEM((NZ, MEM, data), F32),
            pltpu.VMEM((NS, MEM, data), BF16),
            pltpu.VMEM((NS, MEM, data), BF16),
            pltpu.VMEM((NZ, MEM, data), BF16),
            pltpu.VMEM((nob, BLK), F32),
            pltpu.VMEM((4, 16, BLK), BF16),
            pltpu.VMEM((NZ, MEM, data), BF16),
            pltpu.VMEM((NY, NZ, MEM, data), BF16),
            pltpu.VMEM((NS, MEM, cells), BF16),
            pltpu.VMEM((NY, NZ, MEM, cells), BF16),
            pltpu.VMEM((nob, nl, BLK), BF16),
            pltpu.VMEM((2, nl * nob, 128), F32),
            pltpu.VMEM((2, NS, nl // 2, nob, NY * nl), BF16),
            pltpu.VMEM((2, nvb * nl, 128), F32),
            pltpu.VMEM((NZ, MEM, cells), BF16),
            dma((3,)), dma((1,)),
            dma((NX,)), dma((NX,)),
            dma((NX - 1,)), dma((NX - 1,)),
            dma((NS,)), dma((NS,)),
            dma((NS,)), dma((NS,)),
            dma((NS,)), dma(()),
            dma((NY,)), dma((4,)),
            dma((NZ,)), dma((NZ,)),
            dma((NZ,)), dma((NZ,)),
            dma((NZ,)), dma((NZ,)),
            dma((NY,)), dma((NY,)),
            dma((NY, NZ)), dma((NY, NZ)),
            dma((2, NX)), dma((2, NS)),
            dma((2, NX)), dma((2, NS)),
            dma((4, NZ)), dma((4, NS)),
        ],
        compiler_params=pltpu.CompilerParams(
            collective_id=0, has_side_effects=True, vmem_limit_bytes=56 * 1024 * 1024
        ),
        cost_estimate=pl.CostEstimate(flops=900_000_000, bytes_accessed=8_000_000, transcendentals=0),
        name="update",
    )(
        ensemble,
        partials,
        perturb,
        observed.reshape(1, -1),
        variance.reshape(NS, nob, BLK),
        coeff,
    )


def solution(mesh):
    return jax.shard_map(
        local,
        mesh=mesh,
        in_specs=(
            P("mem", "vox"),
            P("vox", "mem", None),
            P("mem", "vox"),
            P("vox"),
            P("vox"),
            P(("vox", "mem"), None),
            P(("vox", "mem"), None),
            P(),
        ),
        out_specs=P("mem", "vox"),
        check_vma=False,
    )
```

```python
import functools

import jax
import jax.numpy as jnp
from jax import lax
from jax.experimental import pallas as pl
from jax.experimental.pallas import tpu as pltpu
from jax.sharding import PartitionSpec as P

MESH = pl.DeviceIdType.MESH
NX, NC, NY, NZ = 4, 2, 4, 8
NS = NX * NC
MEM = 8
BLK = 128
F32, BF16 = jnp.float32, jnp.bfloat16
X1_EARLY = ()


def loop(n, fn):
    lax.fori_loop(0, n, fn, 0)


def kernel(
    ens, par, per, obs, var, lists, tap_i, tap_t, out,
    par_v, per_v, obs_v, lists_v, tap_iv, tap_tv, core_send, core_recv, rs_send, rs_recv, own_sum,
    a0, a1, a2, vh, c0, ch, p1, p_all, x1, x_all, xc, wt, m_f, m_all, comb, ost,
    ld_s,
    co_ss, co_rs, rs_ss, rs_rs, x1_ss, x1_rs, a1_ss, a1_rs, v_ss, v_rs, c_ss, c_rs,
    xz_ss, xz_rs, az_ss, az_rs, pz_ss, pz_rs, py_ss, py_rs, xy_ss, xy_rs, xr_ss, xr_rs,
    mx_ss, mx_rs, mr_ss, mr_rs, mc_ss, mc_rs, o_ss, o_rs,
):
    v = lax.axis_index("vox")
    mem = lax.axis_index("mem")
    x, c = v // NC, lax.rem(v, NC)
    y, z = mem // NZ, lax.rem(mem, NZ)
    oc = 1 - c
    cells = ens.shape[1] // NS
    data = per.shape[1] // NS
    hdata = data // 2
    nob = data // BLK // 2
    nvb = cells // BLK
    nl = NZ * MEM
    nk = NY * nl
    hc = cells // 2

    def dev(vox, yy, zz):
        return (vox, yy * NZ + zz)

    def rc(src, dst, ss, rs, to):
        return pltpu.make_async_remote_copy(
            src_ref=src, dst_ref=dst, send_sem=ss, recv_sem=rs, device_id=to, device_id_type=MESH
        )

    def arrived(ref, sem):
        pltpu.make_async_copy(ref, ref, sem).wait()

    def mod(a, n):
        return lax.rem(a, n)

    partner = dev(NC * x + oc, y, z)

    loads = [
        pltpu.make_async_copy(src, dst, ld_s.at[i])
        for i, (src, dst) in enumerate(
            [(par.at[0], par_v), (per, per_v), (obs, obs_v), (lists, lists_v), (tap_i, tap_iv), (tap_t, tap_tv)]
        )
    ]
    for cp in loads:
        cp.start()

    barrier = pltpu.get_barrier_semaphore()

    def greet(to):
        pl.semaphore_signal(barrier, inc=1, device_id=to, device_id_type=MESH)

    for d in range(1, NS):
        greet(dev(mod(v + d, NS), y, z))
        greet(dev(v, y, mod(z + d, NZ)))
    for d in range(1, NY):
        greet(dev(v, mod(y + d, NY), z))
    home_diag = v == z
    c_to = mem // 4
    c_row = lax.rem(mem, 4)
    for j in range(4):
        src_mem = 4 * v + j
        is_self = jnp.logical_and(home_diag, src_mem == mem)

        @pl.when(jnp.logical_not(is_self))
        def _():
            greet((z, src_mem))

    for s in range(NS):
        is_self = jnp.logical_and(home_diag, v == s)

        @pl.when(jnp.logical_not(is_self))
        def _():
            greet(dev(s, y, v))

    c_self = jnp.logical_and(home_diag, c_to == v)

    loads[0].wait()

    def cast_one(i, carry):
        xx, g = i // NZ, lax.rem(i, NZ)
        for q in range(2):
            col = pl.multiple_of(g * (NS * data) + (NC * xx + oc) * data + q * hdata, hdata)
            core_send[q, xx, g] = par_v[:, pl.ds(col, hdata)].astype(BF16)
        return carry

    loop(NX * NZ, cast_one)
    for cp in loads[1:]:
        cp.wait()
    for s in range(NS):
        a0[s] = (per_v[:, s * data:(s + 1) * data] + obs_v[:, s * data:(s + 1) * data]).astype(BF16)
    tapers = jnp.zeros(tap_iv.shape, F32)
    for t in range(tap_tv.shape[1]):
        tapers += jnp.where(tap_iv[...] == t, tap_tv[:, t:t + 1], 0.0)
    lanes = lax.broadcasted_iota(jnp.int32, (tap_iv.shape[0], BLK), 1)
    coeff = jnp.zeros((tap_iv.shape[0], BLK), F32)
    for j in range(tap_iv.shape[1]):
        coeff += jnp.where(lists_v[:, j:j + 1] == lanes, tapers[:, j:j + 1], 0.0)
    c0[...] = coeff.astype(BF16)

    pl.semaphore_wait(
        barrier,
        (NS - 1) + (NZ - 1) + (NY - 1)
        + 4 - c_self.astype(jnp.int32)
        + NZ - home_diag.astype(jnp.int32),
    )

    sends = []

    def start(cp):
        cp.start()
        sends.append(cp)

    def core_copy(q, e):
        xx = mod(x + e, NX)
        return rc(core_send.at[q, xx], core_recv.at[q, xx], co_ss.at[q, e], co_rs.at[q, xx], partner)

    for q in range(2):
        for e in (2, 1, 3, 0):
            start(core_copy(q, e))

    pltpu.make_async_copy(a0.at[v], a1.at[v], a1_rs.at[v]).start()
    pltpu.make_async_copy(ens.at[:, pl.ds(pl.multiple_of(v * cells, cells), cells)], x1.at[v], x1_rs.at[v]).start()
    for d in range(1, NS):
        to = mod(v + d, NS)
        start(rc(a0.at[to], a1.at[v], a1_ss.at[d], a1_rs.at[v], dev(to, y, z)))

    def send_x1(d):
        to = mod(v + d, NS)
        start(rc(ens.at[:, pl.ds(pl.multiple_of(to * cells, cells), cells)], x1.at[v], x1_ss.at[d], x1_rs.at[v], dev(to, y, z)))

    for d in X1_EARLY:
        send_x1(d)

    @pl.when(home_diag)
    def _():
        pltpu.make_async_copy(var.at[v], vh, v_rs).start()
        for d in range(1, NS):
            to = mod(v + d, NS)
            rc(var.at[to], vh, v_ss.at[d], v_rs, dev(to, y, z)).start()

    for yy in range(NY):
        is_self = jnp.logical_and(c_self, y == yy)

        @pl.when(is_self)
        def _():
            pltpu.make_async_copy(c0, ch.at[c_row], c_rs.at[c_row]).start()

        @pl.when(jnp.logical_not(is_self))
        def _():
            rc(c0, ch.at[c_row], c_ss.at[yy], c_rs.at[c_row], dev(c_to, yy, v)).start()

    for q in range(2):
        for e in (2, 1, 3, 0):
            xx = mod(x + e, NX)
            core_copy(q, e).wait_recv()

            def sum_one(g, carry):
                col = pl.multiple_of(g * (NS * data) + (NC * xx + c) * data + q * hdata, hdata)
                total = par_v[:, pl.ds(col, hdata)] + core_recv[q, xx, g].astype(F32)
                if e == 0:
                    own_sum[q, g] = total
                else:
                    rs_send[q, e - 1, g] = total.astype(BF16)
                return carry

            loop(NZ, sum_one)
            if e:
                start(rc(rs_send.at[q, e - 1], rs_recv.at[q, e - 1], rs_ss.at[q, e - 1], rs_rs.at[q, e - 1], dev(NC * xx + c, y, z)))

    for d in range(1, NS):
        if d not in X1_EARLY:
            send_x1(d)

    def forward_a(d):
        g = mod(z + d, NZ)
        arrived(a1.at[g], a1_rs.at[g])
        if d == 0:
            pltpu.make_async_copy(a1.at[g], a2.at[z], az_rs.at[z]).start()
        else:
            start(rc(a1.at[g], a2.at[z], az_ss.at[d], az_rs.at[z], dev(v, y, g)))

    def forward_x(d):
        g = mod(z + d, NZ)
        arrived(x1.at[g], x1_rs.at[g])
        if d == 0:
            pltpu.make_async_copy(x1.at[g], x_all.at[y, z], xz_rs.at[z]).start()
        else:
            start(rc(x1.at[g], x_all.at[y, z], xz_ss.at[d], xz_rs.at[z], dev(v, y, g)))

    def predict(q):
        for e in range(1, NX):
            rc(rs_send.at[q, e - 1], rs_recv.at[q, e - 1], rs_ss.at[q, e - 1], rs_rs.at[q, e - 1], partner).wait_recv()

        def pred_one(g, carry):
            total = own_sum[q, g]
            for e in range(NX - 1):
                total += rs_recv[q, e, g].astype(F32)
            p1[q, g] = total.astype(BF16)
            return carry

        loop(NZ, pred_one)
        pltpu.make_async_copy(p1.at[q, z], p_all.at[q, y, z], pz_rs.at[q, z]).start()
        for d in range(1, NZ):
            g = mod(z + d, NZ)
            start(rc(p1.at[q, g], p_all.at[q, y, z], pz_ss.at[q, d], pz_rs.at[q, z], dev(v, y, g)))

    def spread_p(q):
        for e in range(NZ):
            zs = mod(z + NZ - e, NZ)
            arrived(p_all.at[q, y, zs], pz_rs.at[q, zs])
        for d in (2, 1, 3):
            start(rc(p_all.at[q, y], p_all.at[q, y], py_ss.at[q, d], py_rs.at[q, y], dev(v, mod(y + d, NY), z)))

    ylo, yhi = mod(y + NY - 1, NY), mod(y + 1, NY)

    def spread_x(e):
        zs = mod(z + NZ - e, NZ)
        arrived(x_all.at[y, zs], xz_rs.at[zs])
        for i, yy in enumerate((yhi, ylo)):
            start(rc(x_all.at[y, zs], x_all.at[y, zs], xy_ss.at[i, e], xy_rs.at[y, zs], dev(v, yy, z)))

    def relay_x(e):
        zs = mod(z + NZ - e, NZ)
        for i, (src, to) in enumerate(((ylo, yhi), (yhi, ylo))):
            arrived(x_all.at[src, zs], xy_rs.at[src, zs])
            part = x_all.at[src, zs, :, pl.ds(i * hc, hc)]
            start(rc(part, part, xr_ss.at[i, e], xr_rs.at[i, zs], dev(v, to, z)))

    def settle_x(e):
        zs = mod(z + NZ - e, NZ)
        yo = mod(y + 2, NY)
        for i in range(2):
            arrived(x_all.at[yo, zs, :, pl.ds(i * hc, hc)], xr_rs.at[i, zs])

    def settle_a():
        for e in range(NZ):
            zs = mod(z + NZ - e, NZ)
            arrived(a2.at[zs], az_rs.at[zs])
        arrived(vh, v_rs)

    def weigh(q):
        def weight_one(o, carry):
            col = pl.ds(pl.multiple_of(o * BLK, BLK), BLK)
            acol = pl.ds(pl.multiple_of(q * hdata + o * BLK, BLK), BLK)
            innov = a2[:, :, acol].astype(F32) - p_all[q, y, :, :, col].astype(F32)
            w = innov.reshape(nl, BLK) / vh[pl.ds(q * nob + o, 1), :]
            wt[q * nob + o] = w.astype(BF16)
            return carry

        loop(nob, weight_one)

    hl = nl // 4

    def moments(q):
        for d in range(1, NY):
            ys = mod(y + d, NY)
            arrived(p_all.at[q, ys], py_rs.at[q, ys])

        def moment_one(o, carry):
            col = pl.ds(pl.multiple_of(o * BLK, BLK), BLK)
            pred = p_all[q, :, :, :, col].astype(F32).reshape(nk, BLK).astype(BF16)
            mom = lax.dot_general(wt[q * nob + o], pred, (((1,), (1,)), ((), ())), preferred_element_type=F32)
            mom = mom - jnp.mean(mom, axis=1, keepdims=True)
            for h in range(2):
                m_f[h, pl.ds(o, nl, stride=nob), :] = mom[:, h * 128:(h + 1) * 128]
            return carry

        loop(nob, moment_one)
        for k in range(2):
            def cast_m(i, carry):
                rows = pl.ds(pl.multiple_of((k * hl + i) * 2 * nob, 2 * nob), 2 * nob)
                for h in range(2):
                    m_all[q, k, v, i, :, h * 128:(h + 1) * 128] = m_f[h, rows, :].astype(BF16)
                return carry

            loop(hl, cast_m)
            mine = m_all.at[q, k, v]
            for i, e in enumerate((1, 3)):
                start(rc(mine, mine, mx_ss.at[q, k, i], mx_rs.at[q, k, v], dev(mod(v + NC * e, NS), y, z)))
            start(rc(mine, mine, mc_ss.at[q, k, 0], mc_rs.at[q, k, v], partner))

    def relay_m(q, k):
        lo, hi = mod(v + NC * 3, NS), mod(v + NC, NS)
        for i, (src, to) in enumerate(((lo, hi), (hi, lo))):
            arrived(m_all.at[q, k, src], mx_rs.at[q, k, src])
            part = m_all.at[q, k, src, pl.ds(i * (hl // 2), hl // 2)]
            start(rc(part, part, mr_ss.at[q, k, i], mr_rs.at[q, k, i], dev(to, y, z)))
            whole = m_all.at[q, k, src]
            start(rc(whole, whole, mc_ss.at[q, k, 1 + i], mc_rs.at[q, k, src], partner))

    def finish_m(q, k):
        far = mod(v + NC * 2, NS)
        for i in range(2):
            arrived(m_all.at[q, k, far, pl.ds(i * (hl // 2), hl // 2)], mr_rs.at[q, k, i])
        whole = m_all.at[q, k, far]
        start(rc(whole, whole, mc_ss.at[q, k, 3], mc_rs.at[q, k, far], partner))

    def settle_m(q, k):
        for e in range(NX):
            vs = NC * mod(x + e, NX) + oc
            arrived(m_all.at[q, k, vs], mc_rs.at[q, k, vs])

    def spread_coeff():
        for j in range(4):
            arrived(ch.at[j], c_rs.at[j])
        rows = lax.broadcasted_iota(jnp.int32, (BLK, 2 * BLK), 0)
        cols = lax.broadcasted_iota(jnp.int32, (BLK, 2 * BLK), 1)
        block = lax.rem(cols // (2 * nob), NS) * (2 * nob) + (cols // BLK) * nob + lax.rem(cols, nob)
        tap = ch[...].reshape(nvb, BLK)
        res = []
        for parity in range(2):
            pick = jnp.logical_and(rows == block, lax.rem(cols // nob, 2) == parity)
            res.append(jnp.dot(tap, jnp.where(pick, 1.0, 0.0).astype(BF16), preferred_element_type=F32))
        return jnp.concatenate(res, axis=0).astype(BF16)

    def combine(coeff, k):
        def combine_one(i, carry):
            mom = m_all[:, k, :, i].reshape(2 * NS * 2 * nob, nk)
            com = jnp.dot(coeff, mom, preferred_element_type=F32)
            for parity in range(2):
                rows = pl.ds((k * hl + i) * 2 + parity, nvb, stride=nl)
                for h in range(2):
                    comb[h, rows, :] = com[parity * nvb:(parity + 1) * nvb, h * 128:(h + 1) * 128]
            return carry

        loop(hl, combine_one)

    def centre():
        def centre_one(b, carry):
            col = pl.ds(pl.multiple_of(b * BLK, BLK), BLK)
            state = x_all[:, :, :, col].astype(F32).reshape(nk, BLK)
            xc[b] = (state - jnp.mean(state, axis=0, keepdims=True)).astype(BF16)
            return carry

        loop(nvb, centre_one)

    parts = 4
    per_part = nvb // parts
    width = per_part * BLK

    def update(q):
        def update_one(i, carry):
            b = q * per_part + i
            col = pl.ds(pl.multiple_of(b * BLK, BLK), BLK)
            rows = pl.ds(pl.multiple_of(b * nl, nl), nl)
            left = jnp.concatenate([comb[h, rows, :].astype(BF16) for h in range(2)], axis=1)
            inc = jnp.dot(left, xc[b], preferred_element_type=F32)
            own = x_all[y, :, :, col].astype(F32)
            ost[:, :, col] = (own + inc.reshape(NZ, MEM, BLK) * (1.0 / (nk - 1))).astype(BF16)
            return carry

        loop(per_part, update_one)
        src_col = pl.ds(q * width, width)
        dst_col = pl.ds(pl.multiple_of(v * cells + q * width, width), width)
        for d in range(NZ):
            zt = mod(z + d, NZ)
            src, dst = ost.at[zt, :, src_col], out.at[:, dst_col]
            if d == 0:
                @pl.when(home_diag)
                def _():
                    pltpu.make_async_copy(src, dst, o_rs.at[q, v]).start()

                @pl.when(jnp.logical_not(home_diag))
                def _():
                    rc(src, dst, o_ss.at[q, 0], o_rs.at[q, v], dev(z, y, zt)).start()
            else:
                start(rc(src, dst, o_ss.at[q, d], o_rs.at[q, v], dev(z, y, zt)))

    for d in range(NZ):
        forward_a(d)
    predict(0)
    predict(1)
    for d in range(4):
        forward_x(d)
    spread_p(0)
    for d in range(4, NZ):
        forward_x(d)
    spread_p(1)
    settle_a()
    weigh(0)
    weigh(1)
    for e in range(2):
        spread_x(e)
    moments(0)
    for e in range(2, 4):
        spread_x(e)
    moments(1)
    for e in range(4, NZ):
        spread_x(e)
    coeff = spread_coeff()
    for i, (q, k) in enumerate(((0, 0), (0, 1), (1, 0), (1, 1))):
        relay_x(2 * i)
        relay_m(q, k)
        relay_x(2 * i + 1)
        finish_m(q, k)
    settle_m(0, 0)
    settle_m(1, 0)
    combine(coeff, 0)
    settle_m(0, 1)
    settle_m(1, 1)
    combine(coeff, 1)
    for e in range(NZ):
        settle_x(e)
    centre()
    for q in range(parts):
        update(q)

    for cp in sends:
        cp.wait_send()

    @pl.when(home_diag)
    def _():
        for d in range(1, NS):
            rc(var.at[0], vh, v_ss.at[d], v_rs, partner).wait_send()

    for yy in range(NY):
        @pl.when(jnp.logical_not(jnp.logical_and(c_self, y == yy)))
        def _():
            rc(c0, ch.at[c_row], c_ss.at[yy], c_rs.at[c_row], partner).wait_send()

    @pl.when(jnp.logical_not(home_diag))
    def _():
        for q in range(parts):
            rc(ost.at[0, :, pl.ds(0, width)], out.at[:, pl.ds(0, width)], o_ss.at[q, 0], o_rs.at[q, v], partner).wait_send()

    for q in range(parts):
        for s in range(NS):
            dst_col = pl.ds(s * cells + q * width, width)
            arrived(out.at[:, dst_col], o_rs.at[q, s])


def local(ensemble, partials, perturb, observed, variance, obs_lists, taper_index, taper_table):
    cells = ensemble.shape[1] // NS
    data = perturb.shape[1] // NS
    nob = data // BLK
    nl = NZ * MEM
    nvb = cells // BLK
    hdata = data // 2
    dma = pltpu.SemaphoreType.DMA
    return pl.pallas_call(
        kernel,
        out_shape=jax.ShapeDtypeStruct(ensemble.shape, BF16),
        in_specs=[pl.BlockSpec(memory_space=pl.ANY)] * 8,
        out_specs=pl.BlockSpec(memory_space=pl.ANY),
        scratch_shapes=[
            pltpu.VMEM(partials.shape[1:], F32),
            pltpu.VMEM(perturb.shape, F32),
            pltpu.VMEM((1, observed.shape[0]), F32),
            pltpu.VMEM(obs_lists.shape, jnp.int32),
            pltpu.VMEM(taper_index.shape, jnp.int32),
            pltpu.VMEM((1, taper_table.shape[0]), F32),
            pltpu.VMEM((2, NX, NZ, MEM, hdata), BF16),
            pltpu.VMEM((2, NX, NZ, MEM, hdata), BF16),
            pltpu.VMEM((2, NX - 1, NZ, MEM, hdata), BF16),
            pltpu.VMEM((2, NX - 1, NZ, MEM, hdata), BF16),
            pltpu.VMEM((2, NZ, MEM, hdata), F32),
            pltpu.VMEM((NS, MEM, data), BF16),
            pltpu.VMEM((NS, MEM, data), BF16),
            pltpu.VMEM((NZ, MEM, data), BF16),
            pltpu.VMEM((nob, BLK), F32),
            pltpu.VMEM((16, BLK), BF16),
            pltpu.VMEM((4, 16, BLK), BF16),
            pltpu.VMEM((2, NZ, MEM, hdata), BF16),
            pltpu.VMEM((2, NY, NZ, MEM, hdata), BF16),
            pltpu.VMEM((NS, MEM, cells), BF16),
            pltpu.VMEM((NY, NZ, MEM, cells), BF16),
            pltpu.VMEM((nvb, NY * nl, BLK), BF16),
            pltpu.VMEM((nob, nl, BLK), BF16),
            pltpu.VMEM((2, nl * nob // 2, 128), F32),
            pltpu.VMEM((2, 2, NS, nl // 4, nob, NY * nl), BF16),
            pltpu.VMEM((2, nvb * nl, 128), F32),
            pltpu.VMEM((NZ, MEM, cells), BF16),
            dma((6,)),
            dma((2, NX)), dma((2, NX)),
            dma((2, NX - 1)), dma((2, NX - 1)),
            dma((NS,)), dma((NS,)),
            dma((NS,)), dma((NS,)),
            dma((NS,)), dma(()),
            dma((NY,)), dma((4,)),
            dma((NZ,)), dma((NZ,)),
            dma((NZ,)), dma((NZ,)),
            dma((2, NZ)), dma((2, NZ)),
            dma((2, NY)), dma((2, NY)),
            dma((2, NZ)), dma((NY, NZ)),
            dma((2, NZ)), dma((2, NZ)),
            dma((2, 2, 2)), dma((2, 2, NS)),
            dma((2, 2, 2)), dma((2, 2, 2)),
            dma((2, 2, 4)), dma((2, 2, NS)),
            dma((4, NZ)), dma((4, NS)),
        ],
        compiler_params=pltpu.CompilerParams(
            collective_id=0, has_side_effects=True, vmem_limit_bytes=58 * 1024 * 1024
        ),
        cost_estimate=pl.CostEstimate(flops=900_000_000, bytes_accessed=8_000_000, transcendentals=0),
        name="update",
    )(
        ensemble,
        partials,
        perturb,
        observed.reshape(1, -1),
        variance.reshape(NS, nob, BLK),
        obs_lists,
        taper_index,
        taper_table.reshape(1, -1),
    )


def solution(mesh):
    return jax.shard_map(
        local,
        mesh=mesh,
        in_specs=(
            P("mem", "vox"),
            P("vox", "mem", None),
            P("mem", "vox"),
            P("vox"),
            P("vox"),
            P(("vox", "mem"), None),
            P(("vox", "mem"), None),
            P(),
        ),
        out_specs=P("mem", "vox"),
        check_vma=False,
    )
```

```python
import functools

import jax
import jax.numpy as jnp
from jax import lax
from jax.experimental import pallas as pl
from jax.experimental.pallas import tpu as pltpu
from jax.sharding import PartitionSpec as P

MESH = pl.DeviceIdType.MESH
NX, NC, NY, NZ = 4, 2, 4, 8
NS = NX * NC
MEM = 8
BLK = 128
F32, BF16 = jnp.float32, jnp.bfloat16
PARTS = 4
EARLY = 0


def loop(n, fn, unroll=1):

    def body(i, carry):
        for r in range(unroll):
            fn(i * unroll + r, carry)
        return carry

    lax.fori_loop(0, n // unroll, body, 0)


def kernel(
    ens, par, per, obs, var, lists, tap_i, tap_t, out,
    par_v, per_v, obs_v, lists_v, tap_iv, tap_tv, core_send, core_recv, rs_send, rs_recv, own_sum,
    a0, a1, a2, vh, c0, ch, p1, p_all, x1, x_all, xc, wt, m_f, m_all, comb, ost,
    ld_s,
    co_ss, co_rs, rs_ss, rs_rs, x1_ss, x1_rs, a1_ss, a1_rs, v_ss, v_rs, c_ss, c_rs,
    xz_ss, xz_rs, az_ss, az_rs, pz_ss, pz_rs, py_ss, py_rs, xy_ss, xy_rs, xr_ss, xr_rs,
    mx_ss, mx_rs, mr_ss, mr_rs, mc_ss, mc_rs, o_ss, o_rs,
):
    v = lax.axis_index("vox")
    mem = lax.axis_index("mem")
    x, c = v // NC, lax.rem(v, NC)
    y, z = mem // NZ, lax.rem(mem, NZ)
    oc = 1 - c
    cells = ens.shape[1] // NS
    data = per.shape[1] // NS
    hdata = data // 2
    nob = data // BLK // 2
    nvb = cells // BLK
    nl = NZ * MEM
    nk = NY * nl
    width = cells // PARTS
    per_part = nvb // PARTS
    hz = NZ // 2

    def dev(vox, yy, zz):
        return (vox, yy * NZ + zz)

    def rc(src, dst, ss, rs, to):
        return pltpu.make_async_remote_copy(
            src_ref=src, dst_ref=dst, send_sem=ss, recv_sem=rs, device_id=to, device_id_type=MESH
        )

    def arrived(ref, sem):
        pltpu.make_async_copy(ref, ref, sem).wait()

    def mod(a, n):
        return lax.rem(a, n)

    partner = dev(NC * x + oc, y, z)

    loads = [
        pltpu.make_async_copy(src, dst, ld_s.at[i])
        for i, (src, dst) in enumerate(
            [(par.at[0], par_v), (per, per_v), (obs, obs_v), (lists, lists_v), (tap_i, tap_iv), (tap_t, tap_tv)]
        )
    ]
    for cp in loads:
        cp.start()

    barrier = pltpu.get_barrier_semaphore()

    def greet(to):
        pl.semaphore_signal(barrier, inc=1, device_id=to, device_id_type=MESH)

    for d in range(1, NS):
        greet(dev(mod(v + d, NS), y, z))
        greet(dev(v, y, mod(z + d, NZ)))
    for d in range(1, NY):
        greet(dev(v, mod(y + d, NY), z))
    home_diag = v == z
    c_to = mem // 4
    c_row = lax.rem(mem, 4)
    for j in range(4):
        src_mem = 4 * v + j
        is_self = jnp.logical_and(home_diag, src_mem == mem)

        @pl.when(jnp.logical_not(is_self))
        def _():
            greet((z, src_mem))

    for s in range(NS):
        is_self = jnp.logical_and(home_diag, v == s)

        @pl.when(jnp.logical_not(is_self))
        def _():
            greet(dev(s, y, v))

    c_self = jnp.logical_and(home_diag, c_to == v)

    loads[0].wait()

    def cast_one(i, carry):
        xx, g = i // NZ, lax.rem(i, NZ)
        for q in range(2):
            col = pl.multiple_of(g * (NS * data) + (NC * xx + oc) * data + q * hdata, hdata)
            core_send[q, xx, g] = par_v[:, pl.ds(col, hdata)].astype(BF16)
        return carry

    loop(NX * NZ, cast_one, 2)
    for cp in loads[1:]:
        cp.wait()
    for s in range(NS):
        a0[s] = (per_v[:, s * data:(s + 1) * data] + obs_v[:, s * data:(s + 1) * data]).astype(BF16)
    tapers = jnp.zeros(tap_iv.shape, F32)
    for t in range(tap_tv.shape[1]):
        tapers += jnp.where(tap_iv[...] == t, tap_tv[:, t:t + 1], 0.0)
    lanes = lax.broadcasted_iota(jnp.int32, (tap_iv.shape[0], BLK), 1)
    coeff = jnp.zeros((tap_iv.shape[0], BLK), F32)
    for j in range(tap_iv.shape[1]):
        coeff += jnp.where(lists_v[:, j:j + 1] == lanes, tapers[:, j:j + 1], 0.0)
    c0[...] = coeff.astype(BF16)

    pl.semaphore_wait(
        barrier,
        (NS - 1) + (NZ - 1) + (NY - 1)
        + 4 - c_self.astype(jnp.int32)
        + NZ - home_diag.astype(jnp.int32),
    )

    sends = []

    def start(cp):
        cp.start()
        sends.append(cp)

    def core_copy(q, e):
        xx = mod(x + e, NX)
        return rc(core_send.at[q, xx], core_recv.at[q, xx], co_ss.at[q, e], co_rs.at[q, xx], partner)

    for q in range(2):
        for e in (2, 1, 3, 0):
            start(core_copy(q, e))

    pltpu.make_async_copy(a0.at[v], a1.at[v], a1_rs.at[v]).start()
    for j in range(PARTS):
        own = ens.at[:, pl.ds(pl.multiple_of(v * cells + j * width, width), width)]
        pltpu.make_async_copy(own, x1.at[j, v], x1_rs.at[j, v]).start()
    for d in range(1, NS):
        to = mod(v + d, NS)
        start(rc(a0.at[to], a1.at[v], a1_ss.at[d], a1_rs.at[v], dev(to, y, z)))

    def send_x1(j):
        for d in range(1, NS):
            to = mod(v + d, NS)
            src = ens.at[:, pl.ds(pl.multiple_of(to * cells + j * width, width), width)]
            start(rc(src, x1.at[j, v], x1_ss.at[j, d], x1_rs.at[j, v], dev(to, y, z)))

    for j in range(EARLY):
        send_x1(j)

    @pl.when(home_diag)
    def _():
        pltpu.make_async_copy(var.at[v], vh, v_rs).start()
        for d in range(1, NS):
            to = mod(v + d, NS)
            rc(var.at[to], vh, v_ss.at[d], v_rs, dev(to, y, z)).start()

    for yy in range(NY):
        is_self = jnp.logical_and(c_self, y == yy)

        @pl.when(is_self)
        def _():
            pltpu.make_async_copy(c0, ch.at[c_row], c_rs.at[c_row]).start()

        @pl.when(jnp.logical_not(is_self))
        def _():
            rc(c0, ch.at[c_row], c_ss.at[yy], c_rs.at[c_row], dev(c_to, yy, v)).start()

    for q in range(2):
        for e in (2, 1, 3, 0):
            xx = mod(x + e, NX)
            core_copy(q, e).wait_recv()

            def sum_one(g, carry):
                col = pl.multiple_of(g * (NS * data) + (NC * xx + c) * data + q * hdata, hdata)
                total = par_v[:, pl.ds(col, hdata)] + core_recv[q, xx, g].astype(F32)
                if e == 0:
                    own_sum[q, g] = total
                else:
                    rs_send[q, e - 1, g] = total.astype(BF16)
                return carry

            loop(NZ, sum_one, 2)
            if e:
                start(rc(rs_send.at[q, e - 1], rs_recv.at[q, e - 1], rs_ss.at[q, e - 1], rs_rs.at[q, e - 1], dev(NC * xx + c, y, z)))

    for j in range(EARLY, PARTS):
        send_x1(j)

    def forward_a(d):
        g = mod(z + d, NZ)
        arrived(a1.at[g], a1_rs.at[g])
        if d == 0:
            pltpu.make_async_copy(a1.at[g], a2.at[z], az_rs.at[z]).start()
        else:
            start(rc(a1.at[g], a2.at[z], az_ss.at[d], az_rs.at[z], dev(v, y, g)))

    def forward_x(j):
        for d in range(NZ):
            g = mod(z + d, NZ)
            arrived(x1.at[j, g], x1_rs.at[j, g])
            if d == 0:
                pltpu.make_async_copy(x1.at[j, g], x_all.at[j, y, z], xz_rs.at[j, z]).start()
            else:
                start(rc(x1.at[j, g], x_all.at[j, y, z], xz_ss.at[j, d], xz_rs.at[j, z], dev(v, y, g)))

    def predict(q):
        for e in range(1, NX):
            rc(rs_send.at[q, e - 1], rs_recv.at[q, e - 1], rs_ss.at[q, e - 1], rs_rs.at[q, e - 1], partner).wait_recv()

        def pred_one(g, carry):
            total = own_sum[q, g]
            for e in range(NX - 1):
                total += rs_recv[q, e, g].astype(F32)
            p1[q, g] = total.astype(BF16)
            return carry

        loop(NZ, pred_one, 2)
        pltpu.make_async_copy(p1.at[q, z], p_all.at[q, y, z], pz_rs.at[q, z]).start()
        for d in range(1, NZ):
            g = mod(z + d, NZ)
            start(rc(p1.at[q, g], p_all.at[q, y, z], pz_ss.at[q, d], pz_rs.at[q, z], dev(v, y, g)))

    def spread_p(q):
        for e in range(NZ):
            zs = mod(z + NZ - e, NZ)
            arrived(p_all.at[q, y, zs], pz_rs.at[q, zs])
        for d in (2, 1, 3):
            start(rc(p_all.at[q, y], p_all.at[q, y], py_ss.at[q, d], py_rs.at[q, y], dev(v, mod(y + d, NY), z)))

    ylo, yhi = mod(y + NY - 1, NY), mod(y + 1, NY)

    def spread_x(j):
        for e in range(NZ):
            zs = mod(z + NZ - e, NZ)
            arrived(x_all.at[j, y, zs], xz_rs.at[j, zs])
        for i, yy in enumerate((yhi, ylo)):
            start(rc(x_all.at[j, y], x_all.at[j, y], xy_ss.at[j, i], xy_rs.at[j, y], dev(v, yy, z)))

    def relay_x(j):
        for i, (src, to) in enumerate(((ylo, yhi), (yhi, ylo))):
            arrived(x_all.at[j, src], xy_rs.at[j, src])
            part = x_all.at[j, src, pl.ds(i * hz, hz)]
            start(rc(part, part, xr_ss.at[j, i], xr_rs.at[j, i], dev(v, to, z)))

    def settle_x(j):
        for i in range(2):
            arrived(x_all.at[j, mod(y + 2, NY), pl.ds(i * hz, hz)], xr_rs.at[j, i])

    def settle_a():
        for e in range(NZ):
            zs = mod(z + NZ - e, NZ)
            arrived(a2.at[zs], az_rs.at[zs])
        arrived(vh, v_rs)

    def weigh(q):
        def weight_one(o, carry):
            col = pl.ds(pl.multiple_of(o * BLK, BLK), BLK)
            acol = pl.ds(pl.multiple_of(q * hdata + o * BLK, BLK), BLK)
            innov = a2[:, :, acol].astype(F32) - p_all[q, y, :, :, col].astype(F32)
            w = innov.reshape(nl, BLK) / vh[pl.ds(q * nob + o, 1), :]
            wt[q * nob + o] = w.astype(BF16)
            return carry

        loop(nob, weight_one, 4)

    hl = nl // 4

    def moments(q):
        for d in range(1, NY):
            ys = mod(y + d, NY)
            arrived(p_all.at[q, ys], py_rs.at[q, ys])

        def moment_one(o, carry):
            col = pl.ds(pl.multiple_of(o * BLK, BLK), BLK)
            pred = p_all[q, :, :, :, col].astype(F32).reshape(nk, BLK).astype(BF16)
            mom = lax.dot_general(wt[q * nob + o], pred, (((1,), (1,)), ((), ())), preferred_element_type=F32)
            mom = mom - jnp.mean(mom, axis=1, keepdims=True)
            for h in range(2):
                m_f[h, pl.ds(o, nl, stride=nob), :] = mom[:, h * 128:(h + 1) * 128]
            return carry

        loop(nob, moment_one, 4)
        for k in range(2):
            def cast_m(i, carry):
                rows = pl.ds(pl.multiple_of((k * hl + i) * 2 * nob, 2 * nob), 2 * nob)
                for h in range(2):
                    m_all[q, k, v, i, :, h * 128:(h + 1) * 128] = m_f[h, rows, :].astype(BF16)
                return carry

            loop(hl, cast_m, 4)
            mine = m_all.at[q, k, v]
            for i, e in enumerate((1, 3)):
                start(rc(mine, mine, mx_ss.at[q, k, i], mx_rs.at[q, k, v], dev(mod(v + NC * e, NS), y, z)))
            start(rc(mine, mine, mc_ss.at[q, k, 0], mc_rs.at[q, k, v], partner))

    def relay_m(q, k):
        lo, hi = mod(v + NC * 3, NS), mod(v + NC, NS)
        for i, (src, to) in enumerate(((lo, hi), (hi, lo))):
            arrived(m_all.at[q, k, src], mx_rs.at[q, k, src])
            part = m_all.at[q, k, src, pl.ds(i * (hl // 2), hl // 2)]
            start(rc(part, part, mr_ss.at[q, k, i], mr_rs.at[q, k, i], dev(to, y, z)))
            whole = m_all.at[q, k, src]
            start(rc(whole, whole, mc_ss.at[q, k, 1 + i], mc_rs.at[q, k, src], partner))

    def finish_m(q, k):
        far = mod(v + NC * 2, NS)
        for i in range(2):
            arrived(m_all.at[q, k, far, pl.ds(i * (hl // 2), hl // 2)], mr_rs.at[q, k, i])
        whole = m_all.at[q, k, far]
        start(rc(whole, whole, mc_ss.at[q, k, 3], mc_rs.at[q, k, far], partner))

    def settle_m(q, k):
        for e in range(NX):
            vs = NC * mod(x + e, NX) + oc
            arrived(m_all.at[q, k, vs], mc_rs.at[q, k, vs])

    def spread_coeff():
        for j in range(4):
            arrived(ch.at[j], c_rs.at[j])
        rows = lax.broadcasted_iota(jnp.int32, (BLK, 2 * BLK), 0)
        cols = lax.broadcasted_iota(jnp.int32, (BLK, 2 * BLK), 1)
        block = lax.rem(cols // (2 * nob), NS) * (2 * nob) + (cols // BLK) * nob + lax.rem(cols, nob)
        tap = ch[...].reshape(nvb, BLK)
        res = []
        for parity in range(2):
            pick = jnp.logical_and(rows == block, lax.rem(cols // nob, 2) == parity)
            res.append(jnp.dot(tap, jnp.where(pick, 1.0, 0.0).astype(BF16), preferred_element_type=F32))
        return jnp.concatenate(res, axis=0).astype(BF16)

    def combine(coeff, k):
        def combine_one(i, carry):
            mom = m_all[:, k, :, i].reshape(2 * NS * 2 * nob, nk)
            com = jnp.dot(coeff, mom, preferred_element_type=F32)
            for parity in range(2):
                rows = pl.ds((k * hl + i) * 2 + parity, nvb, stride=nl)
                for h in range(2):
                    comb[h, rows, :] = com[parity * nvb:(parity + 1) * nvb, h * 128:(h + 1) * 128]
            return carry

        loop(hl, combine_one, 4)

    def centre(j):
        def centre_one(b, carry):
            col = pl.ds(pl.multiple_of(b * BLK, BLK), BLK)
            state = x_all[j, :, :, :, col].astype(F32).reshape(nk, BLK)
            xc[j * per_part + b] = (state - jnp.mean(state, axis=0, keepdims=True)).astype(BF16)
            return carry

        loop(per_part, centre_one, 4)

    def update(j):
        def update_one(b, carry):
            col = pl.ds(pl.multiple_of(b * BLK, BLK), BLK)
            rows = pl.ds(pl.multiple_of((j * per_part + b) * nl, nl), nl)
            left = jnp.concatenate([comb[h, rows, :].astype(BF16) for h in range(2)], axis=1)
            inc = jnp.dot(left, xc[j * per_part + b], preferred_element_type=F32)
            own = x_all[j, y, :, :, col].astype(F32)
            ost[j, :, :, col] = (own + inc.reshape(NZ, MEM, BLK) * (1.0 / (nk - 1))).astype(BF16)
            return carry

        loop(per_part, update_one, 4)
        dst = out.at[:, pl.ds(pl.multiple_of(v * cells + j * width, width), width)]
        for d in range(NZ):
            zt = mod(z + d, NZ)
            src = ost.at[j, zt]
            if d == 0:
                @pl.when(home_diag)
                def _():
                    pltpu.make_async_copy(src, dst, o_rs.at[j, v]).start()

                @pl.when(jnp.logical_not(home_diag))
                def _():
                    rc(src, dst, o_ss.at[j, 0], o_rs.at[j, v], dev(z, y, zt)).start()
            else:
                start(rc(src, dst, o_ss.at[j, d], o_rs.at[j, v], dev(z, y, zt)))

    for d in range(NZ):
        forward_a(d)
    predict(0)
    predict(1)
    spread_p(0)
    forward_x(0)
    spread_p(1)
    forward_x(1)
    settle_a()
    weigh(0)
    weigh(1)
    spread_x(0)
    forward_x(2)
    moments(0)
    moments(1)
    forward_x(3)
    spread_x(1)
    relay_x(0)
    spread_x(2)
    relay_x(1)
    coeff = spread_coeff()
    relay_m(0, 0)
    relay_m(0, 1)
    spread_x(3)
    finish_m(0, 0)
    relay_x(2)
    finish_m(0, 1)
    settle_x(0)
    centre(0)
    relay_m(1, 0)
    relay_m(1, 1)
    settle_x(1)
    centre(1)
    finish_m(1, 0)
    finish_m(1, 1)
    settle_m(0, 0)
    settle_m(1, 0)
    combine(coeff, 0)
    relay_x(3)
    settle_m(0, 1)
    settle_m(1, 1)
    combine(coeff, 1)
    update(0)
    update(1)
    settle_x(2)
    centre(2)
    update(2)
    settle_x(3)
    centre(3)
    update(3)

    for cp in sends:
        cp.wait_send()

    @pl.when(home_diag)
    def _():
        for d in range(1, NS):
            rc(var.at[0], vh, v_ss.at[d], v_rs, partner).wait_send()

    for yy in range(NY):
        @pl.when(jnp.logical_not(jnp.logical_and(c_self, y == yy)))
        def _():
            rc(c0, ch.at[c_row], c_ss.at[yy], c_rs.at[c_row], partner).wait_send()

    @pl.when(jnp.logical_not(home_diag))
    def _():
        for j in range(PARTS):
            rc(ost.at[j, 0], ost.at[j, 0], o_ss.at[j, 0], o_rs.at[j, v], partner).wait_send()

    for j in range(PARTS):
        for s in range(NS):
            arrived(out.at[:, pl.ds(s * cells + j * width, width)], o_rs.at[j, s])


def local(ensemble, partials, perturb, observed, variance, obs_lists, taper_index, taper_table):
    cells = ensemble.shape[1] // NS
    data = perturb.shape[1] // NS
    nob = data // BLK
    nl = NZ * MEM
    nvb = cells // BLK
    hdata = data // 2
    width = cells // PARTS
    dma = pltpu.SemaphoreType.DMA
    return pl.pallas_call(
        kernel,
        out_shape=jax.ShapeDtypeStruct(ensemble.shape, BF16),
        in_specs=[pl.BlockSpec(memory_space=pl.ANY)] * 8,
        out_specs=pl.BlockSpec(memory_space=pl.ANY),
        scratch_shapes=[
            pltpu.VMEM(partials.shape[1:], F32),
            pltpu.VMEM(perturb.shape, F32),
            pltpu.VMEM((1, observed.shape[0]), F32),
            pltpu.VMEM(obs_lists.shape, jnp.int32),
            pltpu.VMEM(taper_index.shape, jnp.int32),
            pltpu.VMEM((1, taper_table.shape[0]), F32),
            pltpu.VMEM((2, NX, NZ, MEM, hdata), BF16),
            pltpu.VMEM((2, NX, NZ, MEM, hdata), BF16),
            pltpu.VMEM((2, NX - 1, NZ, MEM, hdata), BF16),
            pltpu.VMEM((2, NX - 1, NZ, MEM, hdata), BF16),
            pltpu.VMEM((2, NZ, MEM, hdata), F32),
            pltpu.VMEM((NS, MEM, data), BF16),
            pltpu.VMEM((NS, MEM, data), BF16),
            pltpu.VMEM((NZ, MEM, data), BF16),
            pltpu.VMEM((nob, BLK), F32),
            pltpu.VMEM((16, BLK), BF16),
            pltpu.VMEM((4, 16, BLK), BF16),
            pltpu.VMEM((2, NZ, MEM, hdata), BF16),
            pltpu.VMEM((2, NY, NZ, MEM, hdata), BF16),
            pltpu.VMEM((PARTS, NS, MEM, width), BF16),
            pltpu.VMEM((PARTS, NY, NZ, MEM, width), BF16),
            pltpu.VMEM((nvb, NY * nl, BLK), BF16),
            pltpu.VMEM((nob, nl, BLK), BF16),
            pltpu.VMEM((2, nl * nob // 2, 128), F32),
            pltpu.VMEM((2, 2, NS, nl // 4, nob, NY * nl), BF16),
            pltpu.VMEM((2, nvb * nl, 128), F32),
            pltpu.VMEM((PARTS, NZ, MEM, width), BF16),
            dma((6,)),
            dma((2, NX)), dma((2, NX)),
            dma((2, NX - 1)), dma((2, NX - 1)),
            dma((PARTS, NS)), dma((PARTS, NS)),
            dma((NS,)), dma((NS,)),
            dma((NS,)), dma(()),
            dma((NY,)), dma((4,)),
            dma((PARTS, NZ)), dma((PARTS, NZ)),
            dma((NZ,)), dma((NZ,)),
            dma((2, NZ)), dma((2, NZ)),
            dma((2, NY)), dma((2, NY)),
            dma((PARTS, 2)), dma((PARTS, NY)),
            dma((PARTS, 2)), dma((PARTS, 2)),
            dma((2, 2, 2)), dma((2, 2, NS)),
            dma((2, 2, 2)), dma((2, 2, 2)),
            dma((2, 2, 4)), dma((2, 2, NS)),
            dma((PARTS, NZ)), dma((PARTS, NS)),
        ],
        compiler_params=pltpu.CompilerParams(
            collective_id=0, has_side_effects=True, vmem_limit_bytes=58 * 1024 * 1024
        ),
        cost_estimate=pl.CostEstimate(flops=900_000_000, bytes_accessed=8_000_000, transcendentals=0),
        name="update",
    )(
        ensemble,
        partials,
        perturb,
        observed.reshape(1, -1),
        variance.reshape(NS, nob, BLK),
        obs_lists,
        taper_index,
        taper_table.reshape(1, -1),
    )


def solution(mesh):
    return jax.shard_map(
        local,
        mesh=mesh,
        in_specs=(
            P("mem", "vox"),
            P("vox", "mem", None),
            P("mem", "vox"),
            P("vox"),
            P("vox"),
            P(("vox", "mem"), None),
            P(("vox", "mem"), None),
            P(),
        ),
        out_specs=P("mem", "vox"),
        check_vma=False,
    )
```

```python
import functools

import jax
import jax.numpy as jnp
from jax import lax
from jax.experimental import pallas as pl
from jax.experimental.pallas import tpu as pltpu
from jax.sharding import PartitionSpec as P

MESH = pl.DeviceIdType.MESH
NX, NC, NY, NZ = 4, 2, 4, 8
NS = NX * NC
MEM = 8
BLK = 128
F32, BF16 = jnp.float32, jnp.bfloat16
PARTS = 4


def loop(n, fn, unroll=1):

    def body(i, carry):
        for r in range(unroll):
            fn(i * unroll + r, carry)
        return carry

    lax.fori_loop(0, n // unroll, body, 0)


def kernel(
    ens, par, per, obs, var, lists, tap_i, tap_t, out,
    par_v, per_v, obs_v, lists_v, tap_iv, tap_tv, core_send, core_recv, rs_send, rs_recv, own_sum,
    a0, a1, a2, vh, c0, ch, p1, p_all, x1, x_all, xc, wt, m_f, m_all, comb, ost,
    ld_s,
    co_ss, co_rs, rs_ss, rs_rs, x1_ss, x1_rs, a1_ss, a1_rs, v_ss, v_rs, c_ss, c_rs,
    xz_ss, xz_rs, az_ss, az_rs, pz_ss, pz_rs, py_ss, py_rs, xy_ss, xy_rs, xr_ss, xr_rs,
    mx_ss, mx_rs, mr_ss, mr_rs, mc_ss, mc_rs, o_ss, o_rs,
):
    v = lax.axis_index("vox")
    mem = lax.axis_index("mem")
    x, c = v // NC, lax.rem(v, NC)
    y, z = mem // NZ, lax.rem(mem, NZ)
    oc = 1 - c
    cells = ens.shape[1] // NS
    data = per.shape[1] // NS
    hdata = data // 2
    nob = data // BLK // 2
    nvb = cells // BLK
    nl = NZ * MEM
    nk = NY * nl
    width = cells // PARTS
    per_part = nvb // PARTS
    hz = NZ // 2

    def dev(vox, yy, zz):
        return (vox, yy * NZ + zz)

    def rc(src, dst, ss, rs, to):
        return pltpu.make_async_remote_copy(
            src_ref=src, dst_ref=dst, send_sem=ss, recv_sem=rs, device_id=to, device_id_type=MESH
        )

    def arrived(ref, sem):
        pltpu.make_async_copy(ref, ref, sem).wait()

    def mod(a, n):
        return lax.rem(a, n)

    partner = dev(NC * x + oc, y, z)

    loads = [
        pltpu.make_async_copy(src, dst, ld_s.at[i])
        for i, (src, dst) in enumerate(
            [(par.at[0], par_v), (per, per_v), (obs, obs_v), (lists, lists_v), (tap_i, tap_iv), (tap_t, tap_tv)]
        )
    ]
    for cp in loads:
        cp.start()

    barrier = pltpu.get_barrier_semaphore()

    def greet(to):
        pl.semaphore_signal(barrier, inc=1, device_id=to, device_id_type=MESH)

    for d in range(1, NS):
        greet(dev(mod(v + d, NS), y, z))
        greet(dev(v, y, mod(z + d, NZ)))
    for d in range(1, NY):
        greet(dev(v, mod(y + d, NY), z))
    home_diag = v == z
    c_to = mem // 4
    c_row = lax.rem(mem, 4)
    for j in range(4):
        src_mem = 4 * v + j
        is_self = jnp.logical_and(home_diag, src_mem == mem)

        @pl.when(jnp.logical_not(is_self))
        def _():
            greet((z, src_mem))

    for s in range(NS):
        is_self = jnp.logical_and(home_diag, v == s)

        @pl.when(jnp.logical_not(is_self))
        def _():
            greet(dev(s, y, v))

    c_self = jnp.logical_and(home_diag, c_to == v)

    loads[0].wait()

    def cast_one(i, carry):
        xx, g = i // NZ, lax.rem(i, NZ)
        for q in range(2):
            col = pl.multiple_of(g * (NS * data) + (NC * xx + oc) * data + q * hdata, hdata)
            core_send[q, xx, g] = par_v[:, pl.ds(col, hdata)].astype(BF16)
        return carry

    loop(NX * NZ, cast_one, 2)
    for cp in loads[1:]:
        cp.wait()
    for s in range(NS):
        a0[s] = (per_v[:, s * data:(s + 1) * data] + obs_v[:, s * data:(s + 1) * data]).astype(BF16)
    tapers = jnp.zeros(tap_iv.shape, F32)
    for t in range(tap_tv.shape[1]):
        tapers += jnp.where(tap_iv[...] == t, tap_tv[:, t:t + 1], 0.0)
    lanes = lax.broadcasted_iota(jnp.int32, (tap_iv.shape[0], BLK), 1)
    coeff = jnp.zeros((tap_iv.shape[0], BLK), F32)
    for j in range(tap_iv.shape[1]):
        coeff += jnp.where(lists_v[:, j:j + 1] == lanes, tapers[:, j:j + 1], 0.0)
    c0[...] = coeff.astype(BF16)

    pl.semaphore_wait(
        barrier,
        (NS - 1) + (NZ - 1) + (NY - 1)
        + 4 - c_self.astype(jnp.int32)
        + NZ - home_diag.astype(jnp.int32),
    )

    sends = []

    def start(cp):
        cp.start()
        sends.append(cp)

    def core_copy(q, e):
        xx = mod(x + e, NX)
        return rc(core_send.at[q, xx], core_recv.at[q, xx], co_ss.at[q, e], co_rs.at[q, xx], partner)

    for q in range(2):
        for e in (2, 1, 3, 0):
            start(core_copy(q, e))

    pltpu.make_async_copy(a0.at[v], a1.at[v], a1_rs.at[v]).start()
    for j in range(PARTS):
        own = ens.at[:, pl.ds(pl.multiple_of(v * cells + j * width, width), width)]
        pltpu.make_async_copy(own, x1.at[j, v], x1_rs.at[j, v]).start()
    for d in range(1, NS):
        to = mod(v + d, NS)
        start(rc(a0.at[to], a1.at[v], a1_ss.at[d], a1_rs.at[v], dev(to, y, z)))

    def send_x1(j):
        for d in range(1, NS):
            to = mod(v + d, NS)
            src = ens.at[:, pl.ds(pl.multiple_of(to * cells + j * width, width), width)]
            start(rc(src, x1.at[j, v], x1_ss.at[j, d], x1_rs.at[j, v], dev(to, y, z)))

    @pl.when(home_diag)
    def _():
        pltpu.make_async_copy(var.at[v], vh, v_rs).start()
        for d in range(1, NS):
            to = mod(v + d, NS)
            rc(var.at[to], vh, v_ss.at[d], v_rs, dev(to, y, z)).start()

    for yy in range(NY):
        is_self = jnp.logical_and(c_self, y == yy)

        @pl.when(is_self)
        def _():
            pltpu.make_async_copy(c0, ch.at[c_row], c_rs.at[c_row]).start()

        @pl.when(jnp.logical_not(is_self))
        def _():
            rc(c0, ch.at[c_row], c_ss.at[yy], c_rs.at[c_row], dev(c_to, yy, v)).start()

    def sums(q):
        for e in (2, 1, 3, 0):
            xx = mod(x + e, NX)
            core_copy(q, e).wait_recv()

            def sum_one(g, carry):
                col = pl.multiple_of(g * (NS * data) + (NC * xx + c) * data + q * hdata, hdata)
                total = par_v[:, pl.ds(col, hdata)] + core_recv[q, xx, g].astype(F32)
                if e == 0:
                    own_sum[q, g] = total
                else:
                    rs_send[q, e - 1, g] = total.astype(BF16)
                return carry

            loop(NZ, sum_one, 2)
            if e:
                start(rc(rs_send.at[q, e - 1], rs_recv.at[q, e - 1], rs_ss.at[q, e - 1], rs_rs.at[q, e - 1], dev(NC * xx + c, y, z)))


    def forward_a(d):
        g = mod(z + d, NZ)
        arrived(a1.at[g], a1_rs.at[g])
        if d == 0:
            pltpu.make_async_copy(a1.at[g], a2.at[z], az_rs.at[z]).start()
        else:
            start(rc(a1.at[g], a2.at[z], az_ss.at[d], az_rs.at[z], dev(v, y, g)))

    def forward_x(j):
        for d in range(NZ):
            g = mod(z + d, NZ)
            arrived(x1.at[j, g], x1_rs.at[j, g])
            if d == 0:
                pltpu.make_async_copy(x1.at[j, g], x_all.at[j, y, z], xz_rs.at[j, z]).start()
            else:
                start(rc(x1.at[j, g], x_all.at[j, y, z], xz_ss.at[j, d], xz_rs.at[j, z], dev(v, y, g)))

    def predict(q):
        for e in range(1, NX):
            rc(rs_send.at[q, e - 1], rs_recv.at[q, e - 1], rs_ss.at[q, e - 1], rs_rs.at[q, e - 1], partner).wait_recv()

        def pred_one(g, carry):
            total = own_sum[q, g]
            for e in range(NX - 1):
                total += rs_recv[q, e, g].astype(F32)
            p1[q, g] = total.astype(BF16)
            return carry

        loop(NZ, pred_one, 2)
        pltpu.make_async_copy(p1.at[q, z], p_all.at[q, y, z], pz_rs.at[q, z]).start()
        for d in range(1, NZ):
            g = mod(z + d, NZ)
            start(rc(p1.at[q, g], p_all.at[q, y, z], pz_ss.at[q, d], pz_rs.at[q, z], dev(v, y, g)))

    def spread_p(q):
        for e in range(NZ):
            zs = mod(z + NZ - e, NZ)
            arrived(p_all.at[q, y, zs], pz_rs.at[q, zs])
        for d in (2, 1, 3):
            start(rc(p_all.at[q, y], p_all.at[q, y], py_ss.at[q, d], py_rs.at[q, y], dev(v, mod(y + d, NY), z)))

    ylo, yhi = mod(y + NY - 1, NY), mod(y + 1, NY)

    def spread_x(j):
        for e in range(NZ):
            zs = mod(z + NZ - e, NZ)
            arrived(x_all.at[j, y, zs], xz_rs.at[j, zs])
        for i, yy in enumerate((yhi, ylo)):
            start(rc(x_all.at[j, y], x_all.at[j, y], xy_ss.at[j, i], xy_rs.at[j, y], dev(v, yy, z)))

    def relay_x(j):
        for i, (src, to) in enumerate(((ylo, yhi), (yhi, ylo))):
            arrived(x_all.at[j, src], xy_rs.at[j, src])
            part = x_all.at[j, src, pl.ds(i * hz, hz)]
            start(rc(part, part, xr_ss.at[j, i], xr_rs.at[j, i], dev(v, to, z)))

    def settle_x(j):
        for i in range(2):
            arrived(x_all.at[j, mod(y + 2, NY), pl.ds(i * hz, hz)], xr_rs.at[j, i])

    def settle_a():
        for e in range(NZ):
            zs = mod(z + NZ - e, NZ)
            arrived(a2.at[zs], az_rs.at[zs])
        arrived(vh, v_rs)

    def weigh(q):
        def weight_one(o, carry):
            col = pl.ds(pl.multiple_of(o * BLK, BLK), BLK)
            acol = pl.ds(pl.multiple_of(q * hdata + o * BLK, BLK), BLK)
            innov = a2[:, :, acol].astype(F32) - p_all[q, y, :, :, col].astype(F32)
            w = innov.reshape(nl, BLK) / vh[pl.ds(q * nob + o, 1), :]
            wt[q * nob + o] = w.astype(BF16)
            return carry

        loop(nob, weight_one, 4)

    hl = nl // 4

    def moments(q):
        for d in range(1, NY):
            ys = mod(y + d, NY)
            arrived(p_all.at[q, ys], py_rs.at[q, ys])

        def moment_one(o, carry):
            col = pl.ds(pl.multiple_of(o * BLK, BLK), BLK)
            pred = p_all[q, :, :, :, col].astype(F32).reshape(nk, BLK).astype(BF16)
            mom = lax.dot_general(wt[q * nob + o], pred, (((1,), (1,)), ((), ())), preferred_element_type=F32)
            mom = mom - jnp.mean(mom, axis=1, keepdims=True)
            for h in range(2):
                m_f[h, pl.ds(o, nl, stride=nob), :] = mom[:, h * 128:(h + 1) * 128]
            return carry

        loop(nob, moment_one, 4)
        for k in range(2):
            def cast_m(i, carry):
                rows = pl.ds(pl.multiple_of((k * hl + i) * 2 * nob, 2 * nob), 2 * nob)
                for h in range(2):
                    m_all[q, k, v, i, :, h * 128:(h + 1) * 128] = m_f[h, rows, :].astype(BF16)
                return carry

            loop(hl, cast_m, 4)
            mine = m_all.at[q, k, v]
            for i, e in enumerate((1, 3)):
                start(rc(mine, mine, mx_ss.at[q, k, i], mx_rs.at[q, k, v], dev(mod(v + NC * e, NS), y, z)))
            start(rc(mine, mine, mc_ss.at[q, k, 0], mc_rs.at[q, k, v], partner))

    def relay_m(q, k):
        lo, hi = mod(v + NC * 3, NS), mod(v + NC, NS)
        for i, (src, to) in enumerate(((lo, hi), (hi, lo))):
            arrived(m_all.at[q, k, src], mx_rs.at[q, k, src])
            part = m_all.at[q, k, src, pl.ds(i * (hl // 2), hl // 2)]
            start(rc(part, part, mr_ss.at[q, k, i], mr_rs.at[q, k, i], dev(to, y, z)))
            whole = m_all.at[q, k, src]
            start(rc(whole, whole, mc_ss.at[q, k, 1 + i], mc_rs.at[q, k, src], partner))

    def finish_m(q, k):
        far = mod(v + NC * 2, NS)
        for i in range(2):
            arrived(m_all.at[q, k, far, pl.ds(i * (hl // 2), hl // 2)], mr_rs.at[q, k, i])
        whole = m_all.at[q, k, far]
        start(rc(whole, whole, mc_ss.at[q, k, 3], mc_rs.at[q, k, far], partner))

    def settle_m(q, k):
        for e in range(NX):
            vs = NC * mod(x + e, NX) + oc
            arrived(m_all.at[q, k, vs], mc_rs.at[q, k, vs])

    def spread_coeff():
        for j in range(4):
            arrived(ch.at[j], c_rs.at[j])
        rows = lax.broadcasted_iota(jnp.int32, (BLK, 2 * BLK), 0)
        cols = lax.broadcasted_iota(jnp.int32, (BLK, 2 * BLK), 1)
        block = lax.rem(cols // (2 * nob), NS) * (2 * nob) + (cols // BLK) * nob + lax.rem(cols, nob)
        tap = ch[...].reshape(nvb, BLK)
        res = []
        for parity in range(2):
            pick = jnp.logical_and(rows == block, lax.rem(cols // nob, 2) == parity)
            res.append(jnp.dot(tap, jnp.where(pick, 1.0, 0.0).astype(BF16), preferred_element_type=F32))
        return jnp.concatenate(res, axis=0).astype(BF16)

    def combine(coeff, k):
        def combine_one(i, carry):
            mom = m_all[:, k, :, i].reshape(2 * NS * 2 * nob, nk)
            com = jnp.dot(coeff, mom, preferred_element_type=F32)
            for parity in range(2):
                rows = pl.ds((k * hl + i) * 2 + parity, nvb, stride=nl)
                for h in range(2):
                    comb[h, rows, :] = com[parity * nvb:(parity + 1) * nvb, h * 128:(h + 1) * 128]
            return carry

        loop(hl, combine_one, 4)

    def centre(j):
        def centre_one(b, carry):
            col = pl.ds(pl.multiple_of(b * BLK, BLK), BLK)
            state = x_all[j, :, :, :, col].astype(F32).reshape(nk, BLK)
            xc[j * per_part + b] = (state - jnp.mean(state, axis=0, keepdims=True)).astype(BF16)
            return carry

        loop(per_part, centre_one, 4)

    def update(j):
        def update_one(b, carry):
            col = pl.ds(pl.multiple_of(b * BLK, BLK), BLK)
            rows = pl.ds(pl.multiple_of((j * per_part + b) * nl, nl), nl)
            left = jnp.concatenate([comb[h, rows, :].astype(BF16) for h in range(2)], axis=1)
            inc = jnp.dot(left, xc[j * per_part + b], preferred_element_type=F32)
            own = x_all[j, y, :, :, col].astype(F32)
            ost[j, :, :, col] = (own + inc.reshape(NZ, MEM, BLK) * (1.0 / (nk - 1))).astype(BF16)
            return carry

        loop(per_part, update_one, 4)
        dst = out.at[:, pl.ds(pl.multiple_of(v * cells + j * width, width), width)]
        for d in range(NZ):
            zt = mod(z + d, NZ)
            src = ost.at[j, zt]
            if d == 0:
                @pl.when(home_diag)
                def _():
                    pltpu.make_async_copy(src, dst, o_rs.at[j, v]).start()

                @pl.when(jnp.logical_not(home_diag))
                def _():
                    rc(src, dst, o_ss.at[j, 0], o_rs.at[j, v], dev(z, y, zt)).start()
            else:
                start(rc(src, dst, o_ss.at[j, d], o_rs.at[j, v], dev(z, y, zt)))

    sums(0)
    sums(1)
    send_x1(0)
    send_x1(1)
    send_x1(2)
    send_x1(3)
    for d in range(NZ):
        forward_a(d)
    predict(0)
    predict(1)
    spread_p(0)
    forward_x(0)
    spread_p(1)
    forward_x(1)
    settle_a()
    weigh(0)
    weigh(1)
    moments(0)
    spread_x(0)
    forward_x(2)
    moments(1)
    forward_x(3)
    spread_x(1)
    relay_x(0)
    relay_m(0, 0)
    relay_m(0, 1)
    finish_m(0, 0)
    finish_m(0, 1)
    settle_m(0, 0)
    spread_x(2)
    relay_x(1)
    relay_m(1, 0)
    relay_m(1, 1)
    finish_m(1, 0)
    finish_m(1, 1)
    coeff = spread_coeff()
    spread_x(3)
    relay_x(2)
    settle_m(1, 0)
    combine(coeff, 0)
    settle_m(0, 1)
    settle_m(1, 1)
    combine(coeff, 1)
    settle_x(0)
    centre(0)
    update(0)
    relay_x(3)
    settle_x(1)
    centre(1)
    update(1)
    settle_x(2)
    centre(2)
    update(2)
    settle_x(3)
    centre(3)
    update(3)

    for cp in sends:
        cp.wait_send()

    @pl.when(home_diag)
    def _():
        for d in range(1, NS):
            rc(var.at[0], vh, v_ss.at[d], v_rs, partner).wait_send()

    for yy in range(NY):
        @pl.when(jnp.logical_not(jnp.logical_and(c_self, y == yy)))
        def _():
            rc(c0, ch.at[c_row], c_ss.at[yy], c_rs.at[c_row], partner).wait_send()

    @pl.when(jnp.logical_not(home_diag))
    def _():
        for j in range(PARTS):
            rc(ost.at[j, 0], ost.at[j, 0], o_ss.at[j, 0], o_rs.at[j, v], partner).wait_send()

    for j in range(PARTS):
        for s in range(NS):
            arrived(out.at[:, pl.ds(s * cells + j * width, width)], o_rs.at[j, s])


def local(ensemble, partials, perturb, observed, variance, obs_lists, taper_index, taper_table):
    cells = ensemble.shape[1] // NS
    data = perturb.shape[1] // NS
    nob = data // BLK
    nl = NZ * MEM
    nvb = cells // BLK
    hdata = data // 2
    width = cells // PARTS
    dma = pltpu.SemaphoreType.DMA
    return pl.pallas_call(
        kernel,
        out_shape=jax.ShapeDtypeStruct(ensemble.shape, BF16),
        in_specs=[pl.BlockSpec(memory_space=pl.ANY)] * 8,
        out_specs=pl.BlockSpec(memory_space=pl.ANY),
        scratch_shapes=[
            pltpu.VMEM(partials.shape[1:], F32),
            pltpu.VMEM(perturb.shape, F32),
            pltpu.VMEM((1, observed.shape[0]), F32),
            pltpu.VMEM(obs_lists.shape, jnp.int32),
            pltpu.VMEM(taper_index.shape, jnp.int32),
            pltpu.VMEM((1, taper_table.shape[0]), F32),
            pltpu.VMEM((2, NX, NZ, MEM, hdata), BF16),
            pltpu.VMEM((2, NX, NZ, MEM, hdata), BF16),
            pltpu.VMEM((2, NX - 1, NZ, MEM, hdata), BF16),
            pltpu.VMEM((2, NX - 1, NZ, MEM, hdata), BF16),
            pltpu.VMEM((2, NZ, MEM, hdata), F32),
            pltpu.VMEM((NS, MEM, data), BF16),
            pltpu.VMEM((NS, MEM, data), BF16),
            pltpu.VMEM((NZ, MEM, data), BF16),
            pltpu.VMEM((nob, BLK), F32),
            pltpu.VMEM((16, BLK), BF16),
            pltpu.VMEM((4, 16, BLK), BF16),
            pltpu.VMEM((2, NZ, MEM, hdata), BF16),
            pltpu.VMEM((2, NY, NZ, MEM, hdata), BF16),
            pltpu.VMEM((PARTS, NS, MEM, width), BF16),
            pltpu.VMEM((PARTS, NY, NZ, MEM, width), BF16),
            pltpu.VMEM((nvb, NY * nl, BLK), BF16),
            pltpu.VMEM((nob, nl, BLK), BF16),
            pltpu.VMEM((2, nl * nob // 2, 128), F32),
            pltpu.VMEM((2, 2, NS, nl // 4, nob, NY * nl), BF16),
            pltpu.VMEM((2, nvb * nl, 128), F32),
            pltpu.VMEM((PARTS, NZ, MEM, width), BF16),
            dma((6,)),
            dma((2, NX)), dma((2, NX)),
            dma((2, NX - 1)), dma((2, NX - 1)),
            dma((PARTS, NS)), dma((PARTS, NS)),
            dma((NS,)), dma((NS,)),
            dma((NS,)), dma(()),
            dma((NY,)), dma((4,)),
            dma((PARTS, NZ)), dma((PARTS, NZ)),
            dma((NZ,)), dma((NZ,)),
            dma((2, NZ)), dma((2, NZ)),
            dma((2, NY)), dma((2, NY)),
            dma((PARTS, 2)), dma((PARTS, NY)),
            dma((PARTS, 2)), dma((PARTS, 2)),
            dma((2, 2, 2)), dma((2, 2, NS)),
            dma((2, 2, 2)), dma((2, 2, 2)),
            dma((2, 2, 4)), dma((2, 2, NS)),
            dma((PARTS, NZ)), dma((PARTS, NS)),
        ],
        compiler_params=pltpu.CompilerParams(
            collective_id=0, has_side_effects=True, vmem_limit_bytes=58 * 1024 * 1024
        ),
        cost_estimate=pl.CostEstimate(flops=900_000_000, bytes_accessed=8_000_000, transcendentals=0),
        name="update",
    )(
        ensemble,
        partials,
        perturb,
        observed.reshape(1, -1),
        variance.reshape(NS, nob, BLK),
        obs_lists,
        taper_index,
        taper_table.reshape(1, -1),
    )


def solution(mesh):
    return jax.shard_map(
        local,
        mesh=mesh,
        in_specs=(
            P("mem", "vox"),
            P("vox", "mem", None),
            P("mem", "vox"),
            P("vox"),
            P("vox"),
            P(("vox", "mem"), None),
            P(("vox", "mem"), None),
            P(),
        ),
        out_specs=P("mem", "vox"),
        check_vma=False,
    )
```

```python
import functools

import jax
import jax.numpy as jnp
from jax import lax
from jax.experimental import pallas as pl
from jax.experimental.pallas import tpu as pltpu
from jax.sharding import PartitionSpec as P

MESH = pl.DeviceIdType.MESH
NX, NC, NY, NZ = 4, 2, 4, 8
NS = NX * NC
MEM = 8
BLK = 128
F32, BF16 = jnp.float32, jnp.bfloat16
PARTS = 4


def loop(n, fn, unroll=1):

    def body(i, carry):
        for r in range(unroll):
            fn(i * unroll + r, carry)
        return carry

    lax.fori_loop(0, n // unroll, body, 0)


def kernel(
    ens, par, per, obs, var, lists, tap_i, tap_t, out,
    par_v, per_v, obs_v, lists_v, tap_iv, tap_tv, core_send, core_recv, rs_send, rs_recv, own_sum,
    a0, a1, a2, vh, c0, ch, p1, p_all, x1, x_all, xc, wt, m_f, m_all, comb, ost,
    ld_s,
    co_ss, co_rs, rs_ss, rs_rs, x1_ss, x1_rs, a1_ss, a1_rs, v_ss, v_rs, c_ss, c_rs,
    xz_ss, xz_rs, az_ss, az_rs, pz_ss, pz_rs, py_ss, py_rs, xy_ss, xy_rs, xr_ss, xr_rs,
    mx_ss, mx_rs, mr_ss, mr_rs, mc_ss, mc_rs, o_ss, o_rs,
):
    v = lax.axis_index("vox")
    mem = lax.axis_index("mem")
    x, c = v // NC, lax.rem(v, NC)
    y, z = mem // NZ, lax.rem(mem, NZ)
    oc = 1 - c
    cells = ens.shape[1] // NS
    data = per.shape[1] // NS
    hdata = data // 2
    nob = data // BLK // 2
    nvb = cells // BLK
    nl = NZ * MEM
    nk = NY * nl
    width = cells // PARTS
    per_part = nvb // PARTS
    hz = NZ // 2

    def dev(vox, yy, zz):
        return (vox, yy * NZ + zz)

    def rc(src, dst, ss, rs, to):
        return pltpu.make_async_remote_copy(
            src_ref=src, dst_ref=dst, send_sem=ss, recv_sem=rs, device_id=to, device_id_type=MESH
        )

    def arrived(ref, sem):
        pltpu.make_async_copy(ref, ref, sem).wait()

    def mod(a, n):
        return lax.rem(a, n)

    partner = dev(NC * x + oc, y, z)

    loads = [
        pltpu.make_async_copy(src, dst, ld_s.at[i])
        for i, (src, dst) in enumerate(
            [(par.at[0], par_v), (per, per_v), (obs, obs_v), (lists, lists_v), (tap_i, tap_iv), (tap_t, tap_tv)]
        )
    ]
    for cp in loads:
        cp.start()

    barrier = pltpu.get_barrier_semaphore()

    def greet(to):
        pl.semaphore_signal(barrier, inc=1, device_id=to, device_id_type=MESH)

    for d in range(1, NS):
        greet(dev(mod(v + d, NS), y, z))
        greet(dev(v, y, mod(z + d, NZ)))
    for d in range(1, NY):
        greet(dev(v, mod(y + d, NY), z))
    home_diag = v == z
    c_to = mem // 4
    c_row = lax.rem(mem, 4)
    for j in range(4):
        src_mem = 4 * v + j
        is_self = jnp.logical_and(home_diag, src_mem == mem)

        @pl.when(jnp.logical_not(is_self))
        def _():
            greet((z, src_mem))

    for s in range(NS):
        is_self = jnp.logical_and(home_diag, v == s)

        @pl.when(jnp.logical_not(is_self))
        def _():
            greet(dev(s, y, v))

    c_self = jnp.logical_and(home_diag, c_to == v)

    loads[0].wait()

    def cast_one(i, carry):
        xx, g = i // NZ, lax.rem(i, NZ)
        for q in range(2):
            col = pl.multiple_of(g * (NS * data) + (NC * xx + oc) * data + q * hdata, hdata)
            core_send[q, xx, g] = par_v[:, pl.ds(col, hdata)].astype(BF16)
        return carry

    loop(NX * NZ, cast_one, 2)
    for cp in loads[1:]:
        cp.wait()
    for s in range(NS):
        a0[s] = (per_v[:, s * data:(s + 1) * data] + obs_v[:, s * data:(s + 1) * data]).astype(BF16)
    tapers = jnp.zeros(tap_iv.shape, F32)
    for t in range(tap_tv.shape[1]):
        tapers += jnp.where(tap_iv[...] == t, tap_tv[:, t:t + 1], 0.0)
    lanes = lax.broadcasted_iota(jnp.int32, (tap_iv.shape[0], BLK), 1)
    coeff = jnp.zeros((tap_iv.shape[0], BLK), F32)
    for j in range(tap_iv.shape[1]):
        coeff += jnp.where(lists_v[:, j:j + 1] == lanes, tapers[:, j:j + 1], 0.0)
    c0[...] = coeff.astype(BF16)

    pl.semaphore_wait(
        barrier,
        (NS - 1) + (NZ - 1) + (NY - 1)
        + 4 - c_self.astype(jnp.int32)
        + NZ - home_diag.astype(jnp.int32),
    )

    sends = []

    def start(cp):
        cp.start()
        sends.append(cp)

    def core_copy(q, e):
        xx = mod(x + e, NX)
        return rc(core_send.at[q, xx], core_recv.at[q, xx], co_ss.at[q, e], co_rs.at[q, xx], partner)

    for q in range(2):
        for e in (2, 1, 3, 0):
            start(core_copy(q, e))

    pltpu.make_async_copy(a0.at[v], a1.at[v], a1_rs.at[v]).start()
    for j in range(PARTS):
        own = ens.at[:, pl.ds(pl.multiple_of(v * cells + j * width, width), width)]
        pltpu.make_async_copy(own, x1.at[j, v], x1_rs.at[j, v]).start()
    for d in range(1, NS):
        to = mod(v + d, NS)
        start(rc(a0.at[to], a1.at[v], a1_ss.at[d], a1_rs.at[v], dev(to, y, z)))

    def send_x1(j):
        for d in range(1, NS):
            to = mod(v + d, NS)
            src = ens.at[:, pl.ds(pl.multiple_of(to * cells + j * width, width), width)]
            start(rc(src, x1.at[j, v], x1_ss.at[j, d], x1_rs.at[j, v], dev(to, y, z)))

    @pl.when(home_diag)
    def _():
        pltpu.make_async_copy(var.at[v], vh, v_rs).start()
        for d in range(1, NS):
            to = mod(v + d, NS)
            rc(var.at[to], vh, v_ss.at[d], v_rs, dev(to, y, z)).start()

    for yy in range(NY):
        is_self = jnp.logical_and(c_self, y == yy)

        @pl.when(is_self)
        def _():
            pltpu.make_async_copy(c0, ch.at[c_row], c_rs.at[c_row]).start()

        @pl.when(jnp.logical_not(is_self))
        def _():
            rc(c0, ch.at[c_row], c_ss.at[yy], c_rs.at[c_row], dev(c_to, yy, v)).start()

    def sums(q):
        for e in (2, 1, 3, 0):
            xx = mod(x + e, NX)
            core_copy(q, e).wait_recv()

            def sum_one(g, carry):
                col = pl.multiple_of(g * (NS * data) + (NC * xx + c) * data + q * hdata, hdata)
                total = par_v[:, pl.ds(col, hdata)] + core_recv[q, xx, g].astype(F32)
                if e == 0:
                    own_sum[q, g] = total
                else:
                    rs_send[q, e - 1, g] = total.astype(BF16)
                return carry

            loop(NZ, sum_one, 2)
            if e:
                start(rc(rs_send.at[q, e - 1], rs_recv.at[q, e - 1], rs_ss.at[q, e - 1], rs_rs.at[q, e - 1], dev(NC * xx + c, y, z)))


    def forward_a(d):
        g = mod(z + d, NZ)
        arrived(a1.at[g], a1_rs.at[g])
        if d == 0:
            pltpu.make_async_copy(a1.at[g], a2.at[z], az_rs.at[z]).start()
        else:
            start(rc(a1.at[g], a2.at[z], az_ss.at[d], az_rs.at[z], dev(v, y, g)))

    def forward_x(j):
        for d in range(NZ):
            g = mod(z + d, NZ)
            arrived(x1.at[j, g], x1_rs.at[j, g])
            if d == 0:
                pltpu.make_async_copy(x1.at[j, g], x_all.at[j, y, z], xz_rs.at[j, z]).start()
            else:
                start(rc(x1.at[j, g], x_all.at[j, y, z], xz_ss.at[j, d], xz_rs.at[j, z], dev(v, y, g)))

    def predict(q):
        for e in range(1, NX):
            rc(rs_send.at[q, e - 1], rs_recv.at[q, e - 1], rs_ss.at[q, e - 1], rs_rs.at[q, e - 1], partner).wait_recv()

        def pred_one(g, carry):
            total = own_sum[q, g]
            for e in range(NX - 1):
                total += rs_recv[q, e, g].astype(F32)
            p1[q, g] = total.astype(BF16)
            return carry

        loop(NZ, pred_one, 2)
        pltpu.make_async_copy(p1.at[q, z], p_all.at[q, y, z], pz_rs.at[q, z]).start()
        for d in range(1, NZ):
            g = mod(z + d, NZ)
            start(rc(p1.at[q, g], p_all.at[q, y, z], pz_ss.at[q, d], pz_rs.at[q, z], dev(v, y, g)))

    def spread_p(q):
        for e in range(NZ):
            zs = mod(z + NZ - e, NZ)
            arrived(p_all.at[q, y, zs], pz_rs.at[q, zs])
        for d in (2, 1, 3):
            start(rc(p_all.at[q, y], p_all.at[q, y], py_ss.at[q, d], py_rs.at[q, y], dev(v, mod(y + d, NY), z)))

    ylo, yhi = mod(y + NY - 1, NY), mod(y + 1, NY)

    def spread_x(j):
        for e in range(NZ):
            zs = mod(z + NZ - e, NZ)
            arrived(x_all.at[j, y, zs], xz_rs.at[j, zs])
        for i, yy in enumerate((yhi, ylo)):
            start(rc(x_all.at[j, y], x_all.at[j, y], xy_ss.at[j, i], xy_rs.at[j, y], dev(v, yy, z)))

    def relay_x(j):
        for i, (src, to) in enumerate(((ylo, yhi), (yhi, ylo))):
            arrived(x_all.at[j, src], xy_rs.at[j, src])
            part = x_all.at[j, src, pl.ds(i * hz, hz)]
            start(rc(part, part, xr_ss.at[j, i], xr_rs.at[j, i], dev(v, to, z)))

    def settle_x(j):
        for i in range(2):
            arrived(x_all.at[j, mod(y + 2, NY), pl.ds(i * hz, hz)], xr_rs.at[j, i])

    def settle_a():
        for e in range(NZ):
            zs = mod(z + NZ - e, NZ)
            arrived(a2.at[zs], az_rs.at[zs])
        arrived(vh, v_rs)

    def weigh(q):
        def weight_one(o, carry):
            col = pl.ds(pl.multiple_of(o * BLK, BLK), BLK)
            acol = pl.ds(pl.multiple_of(q * hdata + o * BLK, BLK), BLK)
            innov = a2[:, :, acol].astype(F32) - p_all[q, y, :, :, col].astype(F32)
            w = innov.reshape(nl, BLK) / vh[pl.ds(q * nob + o, 1), :]
            wt[q * nob + o] = w.astype(BF16)
            return carry

        loop(nob, weight_one, 4)

    hl = nl // 4

    def moments(q):
        for d in range(1, NY):
            ys = mod(y + d, NY)
            arrived(p_all.at[q, ys], py_rs.at[q, ys])

        def moment_one(o, carry):
            col = pl.ds(pl.multiple_of(o * BLK, BLK), BLK)
            pred = p_all[q, :, :, :, col].astype(F32).reshape(nk, BLK).astype(BF16)
            mom = lax.dot_general(wt[q * nob + o], pred, (((1,), (1,)), ((), ())), preferred_element_type=F32)
            mom = mom - jnp.mean(mom, axis=1, keepdims=True)
            for h in range(2):
                m_f[h, pl.ds(o, nl, stride=nob), :] = mom[:, h * 128:(h + 1) * 128]
            return carry

        loop(nob, moment_one, 4)
        for k in range(2):
            def cast_m(i, carry):
                rows = pl.ds(pl.multiple_of((k * hl + i) * 2 * nob, 2 * nob), 2 * nob)
                for h in range(2):
                    m_all[q, k, v, i, :, h * 128:(h + 1) * 128] = m_f[h, rows, :].astype(BF16)
                return carry

            loop(hl, cast_m, 4)
            mine = m_all.at[q, k, v]
            for i, e in enumerate((1, 3)):
                start(rc(mine, mine, mx_ss.at[q, k, i], mx_rs.at[q, k, v], dev(mod(v + NC * e, NS), y, z)))
            start(rc(mine, mine, mc_ss.at[q, k, 0], mc_rs.at[q, k, v], partner))

    def relay_m(q, k):
        lo, hi = mod(v + NC * 3, NS), mod(v + NC, NS)
        for i, (src, to) in enumerate(((lo, hi), (hi, lo))):
            arrived(m_all.at[q, k, src], mx_rs.at[q, k, src])
            part = m_all.at[q, k, src, pl.ds(i * (hl // 2), hl // 2)]
            start(rc(part, part, mr_ss.at[q, k, i], mr_rs.at[q, k, i], dev(to, y, z)))
            whole = m_all.at[q, k, src]
            start(rc(whole, whole, mc_ss.at[q, k, 1 + i], mc_rs.at[q, k, src], partner))

    def finish_m(q, k):
        far = mod(v + NC * 2, NS)
        for i in range(2):
            arrived(m_all.at[q, k, far, pl.ds(i * (hl // 2), hl // 2)], mr_rs.at[q, k, i])
        whole = m_all.at[q, k, far]
        start(rc(whole, whole, mc_ss.at[q, k, 3], mc_rs.at[q, k, far], partner))

    def settle_m(q, k):
        for e in range(NX):
            vs = NC * mod(x + e, NX) + oc
            arrived(m_all.at[q, k, vs], mc_rs.at[q, k, vs])

    def spread_coeff():
        for j in range(4):
            arrived(ch.at[j], c_rs.at[j])
        rows = lax.broadcasted_iota(jnp.int32, (BLK, 2 * BLK), 0)
        cols = lax.broadcasted_iota(jnp.int32, (BLK, 2 * BLK), 1)
        block = lax.rem(cols // (2 * nob), NS) * (2 * nob) + (cols // BLK) * nob + lax.rem(cols, nob)
        tap = ch[...].reshape(nvb, BLK)
        res = []
        for parity in range(2):
            pick = jnp.logical_and(rows == block, lax.rem(cols // nob, 2) == parity)
            res.append(jnp.dot(tap, jnp.where(pick, 1.0, 0.0).astype(BF16), preferred_element_type=F32))
        return jnp.concatenate(res, axis=0).astype(BF16)

    def combine(coeff, k):
        def combine_one(i, carry):
            mom = m_all[:, k, :, i].reshape(2 * NS * 2 * nob, nk)
            com = jnp.dot(coeff, mom, preferred_element_type=F32)
            for parity in range(2):
                rows = pl.ds((k * hl + i) * 2 + parity, nvb, stride=nl)
                for h in range(2):
                    comb[h, rows, :] = com[parity * nvb:(parity + 1) * nvb, h * 128:(h + 1) * 128]
            return carry

        loop(hl, combine_one, 4)

    def centre(j):
        def centre_one(b, carry):
            col = pl.ds(pl.multiple_of(b * BLK, BLK), BLK)
            state = x_all[j, :, :, :, col].astype(F32).reshape(nk, BLK)
            xc[j * per_part + b] = (state - jnp.mean(state, axis=0, keepdims=True)).astype(BF16)
            return carry

        loop(per_part, centre_one, 4)

    def update(j):
        def update_one(b, carry):
            col = pl.ds(pl.multiple_of(b * BLK, BLK), BLK)
            rows = pl.ds(pl.multiple_of((j * per_part + b) * nl, nl), nl)
            left = jnp.concatenate([comb[h, rows, :].astype(BF16) for h in range(2)], axis=1)
            inc = jnp.dot(left, xc[j * per_part + b], preferred_element_type=F32)
            own = x_all[j, y, :, :, col].astype(F32)
            ost[j, :, :, col] = (own + inc.reshape(NZ, MEM, BLK) * (1.0 / (nk - 1))).astype(BF16)
            return carry

        loop(per_part, update_one, 4)
        dst = out.at[:, pl.ds(pl.multiple_of(v * cells + j * width, width), width)]
        for d in range(NZ):
            zt = mod(z + d, NZ)
            src = ost.at[j, zt]
            if d == 0:
                @pl.when(home_diag)
                def _():
                    pltpu.make_async_copy(src, dst, o_rs.at[j, v]).start()

                @pl.when(jnp.logical_not(home_diag))
                def _():
                    rc(src, dst, o_ss.at[j, 0], o_rs.at[j, v], dev(z, y, zt)).start()
            else:
                start(rc(src, dst, o_ss.at[j, d], o_rs.at[j, v], dev(z, y, zt)))

    sums(0)
    sums(1)
    send_x1(0)
    send_x1(1)
    send_x1(2)
    send_x1(3)
    for d in range(NZ):
        forward_a(d)
    predict(0)
    predict(1)
    spread_p(0)
    forward_x(0)
    spread_p(1)
    forward_x(1)
    settle_a()
    weigh(0)
    weigh(1)
    moments(0)
    spread_x(0)
    forward_x(2)
    moments(1)
    forward_x(3)
    spread_x(1)
    relay_x(0)
    relay_m(0, 0)
    relay_m(0, 1)
    finish_m(0, 0)
    finish_m(0, 1)
    settle_m(0, 0)
    spread_x(2)
    relay_x(1)
    relay_m(1, 0)
    relay_m(1, 1)
    finish_m(1, 0)
    finish_m(1, 1)
    coeff = spread_coeff()
    spread_x(3)
    relay_x(2)
    settle_x(0)
    centre(0)
    settle_m(1, 0)
    combine(coeff, 0)
    settle_m(0, 1)
    settle_m(1, 1)
    combine(coeff, 1)
    update(0)
    relay_x(3)
    settle_x(1)
    centre(1)
    update(1)
    settle_x(2)
    centre(2)
    update(2)
    settle_x(3)
    centre(3)
    update(3)

    for cp in sends:
        cp.wait_send()

    @pl.when(home_diag)
    def _():
        for d in range(1, NS):
            rc(var.at[0], vh, v_ss.at[d], v_rs, partner).wait_send()

    for yy in range(NY):
        @pl.when(jnp.logical_not(jnp.logical_and(c_self, y == yy)))
        def _():
            rc(c0, ch.at[c_row], c_ss.at[yy], c_rs.at[c_row], partner).wait_send()

    @pl.when(jnp.logical_not(home_diag))
    def _():
        for j in range(PARTS):
            rc(ost.at[j, 0], ost.at[j, 0], o_ss.at[j, 0], o_rs.at[j, v], partner).wait_send()

    for j in range(PARTS):
        for s in range(NS):
            arrived(out.at[:, pl.ds(s * cells + j * width, width)], o_rs.at[j, s])


def local(ensemble, partials, perturb, observed, variance, obs_lists, taper_index, taper_table):
    cells = ensemble.shape[1] // NS
    data = perturb.shape[1] // NS
    nob = data // BLK
    nl = NZ * MEM
    nvb = cells // BLK
    hdata = data // 2
    width = cells // PARTS
    dma = pltpu.SemaphoreType.DMA
    return pl.pallas_call(
        kernel,
        out_shape=jax.ShapeDtypeStruct(ensemble.shape, BF16),
        in_specs=[pl.BlockSpec(memory_space=pl.ANY)] * 8,
        out_specs=pl.BlockSpec(memory_space=pl.ANY),
        scratch_shapes=[
            pltpu.VMEM(partials.shape[1:], F32),
            pltpu.VMEM(perturb.shape, F32),
            pltpu.VMEM((1, observed.shape[0]), F32),
            pltpu.VMEM(obs_lists.shape, jnp.int32),
            pltpu.VMEM(taper_index.shape, jnp.int32),
            pltpu.VMEM((1, taper_table.shape[0]), F32),
            pltpu.VMEM((2, NX, NZ, MEM, hdata), BF16),
            pltpu.VMEM((2, NX, NZ, MEM, hdata), BF16),
            pltpu.VMEM((2, NX - 1, NZ, MEM, hdata), BF16),
            pltpu.VMEM((2, NX - 1, NZ, MEM, hdata), BF16),
            pltpu.VMEM((2, NZ, MEM, hdata), F32),
            pltpu.VMEM((NS, MEM, data), BF16),
            pltpu.VMEM((NS, MEM, data), BF16),
            pltpu.VMEM((NZ, MEM, data), BF16),
            pltpu.VMEM((nob, BLK), F32),
            pltpu.VMEM((16, BLK), BF16),
            pltpu.VMEM((4, 16, BLK), BF16),
            pltpu.VMEM((2, NZ, MEM, hdata), BF16),
            pltpu.VMEM((2, NY, NZ, MEM, hdata), BF16),
            pltpu.VMEM((PARTS, NS, MEM, width), BF16),
            pltpu.VMEM((PARTS, NY, NZ, MEM, width), BF16),
            pltpu.VMEM((nvb, NY * nl, BLK), BF16),
            pltpu.VMEM((nob, nl, BLK), BF16),
            pltpu.VMEM((2, nl * nob // 2, 128), F32),
            pltpu.VMEM((2, 2, NS, nl // 4, nob, NY * nl), BF16),
            pltpu.VMEM((2, nvb * nl, 128), F32),
            pltpu.VMEM((PARTS, NZ, MEM, width), BF16),
            dma((6,)),
            dma((2, NX)), dma((2, NX)),
            dma((2, NX - 1)), dma((2, NX - 1)),
            dma((PARTS, NS)), dma((PARTS, NS)),
            dma((NS,)), dma((NS,)),
            dma((NS,)), dma(()),
            dma((NY,)), dma((4,)),
            dma((PARTS, NZ)), dma((PARTS, NZ)),
            dma((NZ,)), dma((NZ,)),
            dma((2, NZ)), dma((2, NZ)),
            dma((2, NY)), dma((2, NY)),
            dma((PARTS, 2)), dma((PARTS, NY)),
            dma((PARTS, 2)), dma((PARTS, 2)),
            dma((2, 2, 2)), dma((2, 2, NS)),
            dma((2, 2, 2)), dma((2, 2, 2)),
            dma((2, 2, 4)), dma((2, 2, NS)),
            dma((PARTS, NZ)), dma((PARTS, NS)),
        ],
        compiler_params=pltpu.CompilerParams(
            collective_id=0, has_side_effects=True, vmem_limit_bytes=58 * 1024 * 1024
        ),
        cost_estimate=pl.CostEstimate(flops=900_000_000, bytes_accessed=8_000_000, transcendentals=0),
        name="update",
    )(
        ensemble,
        partials,
        perturb,
        observed.reshape(1, -1),
        variance.reshape(NS, nob, BLK),
        obs_lists,
        taper_index,
        taper_table.reshape(1, -1),
    )


def solution(mesh):
    return jax.shard_map(
        local,
        mesh=mesh,
        in_specs=(
            P("mem", "vox"),
            P("vox", "mem", None),
            P("mem", "vox"),
            P("vox"),
            P("vox"),
            P(("vox", "mem"), None),
            P(("vox", "mem"), None),
            P(),
        ),
        out_specs=P("mem", "vox"),
        check_vma=False,
    )
```

```python
import functools

import jax
import jax.numpy as jnp
from jax import lax
from jax.experimental import pallas as pl
from jax.experimental.pallas import tpu as pltpu
from jax.sharding import PartitionSpec as P

MESH = pl.DeviceIdType.MESH
NX, NC, NY, NZ = 4, 2, 4, 8
NS = NX * NC
MEM = 8
BLK = 128
F32, BF16 = jnp.float32, jnp.bfloat16
PARTS = 4


def loop(n, fn, unroll=1):

    def body(i, carry):
        for r in range(unroll):
            fn(i * unroll + r, carry)
        return carry

    lax.fori_loop(0, n // unroll, body, 0)


def kernel(
    ens, par, per, obs, var, lists, tap_i, tap_t, out,
    par_v, per_v, obs_v, lists_v, tap_iv, tap_tv, core_send, core_recv, rs_send, rs_recv, own_sum,
    a0, a1, a2, vh, c0, ch, p1, p_all, x1, x_all, xc, wt, m_f, m_all, comb, ost,
    ld_s,
    co_ss, co_rs, rs_ss, rs_rs, x1_ss, x1_rs, a1_ss, a1_rs, v_ss, v_rs, c_ss, c_rs,
    xz_ss, xz_rs, az_ss, az_rs, pz_ss, pz_rs, py_ss, py_rs, xy_ss, xy_rs, xr_ss, xr_rs,
    mx_ss, mx_rs, mr_ss, mr_rs, mc_ss, mc_rs, o_ss, o_rs,
):
    v = lax.axis_index("vox")
    mem = lax.axis_index("mem")
    x, c = v // NC, lax.rem(v, NC)
    y, z = mem // NZ, lax.rem(mem, NZ)
    oc = 1 - c
    cells = ens.shape[1] // NS
    data = per.shape[1] // NS
    hdata = data // 2
    nob = data // BLK // 2
    nvb = cells // BLK
    nl = NZ * MEM
    nk = NY * nl
    width = cells // PARTS
    per_part = nvb // PARTS
    hz = NZ // 2

    def dev(vox, yy, zz):
        return (vox, yy * NZ + zz)

    def rc(src, dst, ss, rs, to):
        return pltpu.make_async_remote_copy(
            src_ref=src, dst_ref=dst, send_sem=ss, recv_sem=rs, device_id=to, device_id_type=MESH
        )

    def arrived(ref, sem):
        pltpu.make_async_copy(ref, ref, sem).wait()

    def mod(a, n):
        return lax.rem(a, n)

    partner = dev(NC * x + oc, y, z)

    loads = [
        pltpu.make_async_copy(src, dst, ld_s.at[i])
        for i, (src, dst) in enumerate(
            [(par.at[0], par_v), (per, per_v), (obs, obs_v), (lists, lists_v), (tap_i, tap_iv), (tap_t, tap_tv)]
        )
    ]
    for cp in loads:
        cp.start()

    barrier = pltpu.get_barrier_semaphore()

    def greet(to):
        pl.semaphore_signal(barrier, inc=1, device_id=to, device_id_type=MESH)

    for d in range(1, NS):
        greet(dev(mod(v + d, NS), y, z))
        greet(dev(v, y, mod(z + d, NZ)))
    for d in range(1, NY):
        greet(dev(v, mod(y + d, NY), z))
    home_diag = v == z
    c_to = mem // 4
    c_row = lax.rem(mem, 4)
    for j in range(4):
        src_mem = 4 * v + j
        is_self = jnp.logical_and(home_diag, src_mem == mem)

        @pl.when(jnp.logical_not(is_self))
        def _():
            greet((z, src_mem))

    for s in range(NS):
        is_self = jnp.logical_and(home_diag, v == s)

        @pl.when(jnp.logical_not(is_self))
        def _():
            greet(dev(s, y, v))

    c_self = jnp.logical_and(home_diag, c_to == v)

    loads[0].wait()

    def cast_one(i, carry):
        xx, g = i // NZ, lax.rem(i, NZ)
        for q in range(2):
            col = pl.multiple_of(g * (NS * data) + (NC * xx + oc) * data + q * hdata, hdata)
            core_send[q, xx, g] = par_v[:, pl.ds(col, hdata)].astype(BF16)
        return carry

    loop(NX * NZ, cast_one, 2)
    for cp in loads[1:]:
        cp.wait()
    for s in range(NS):
        a0[s] = (per_v[:, s * data:(s + 1) * data] + obs_v[:, s * data:(s + 1) * data]).astype(BF16)
    tapers = jnp.zeros(tap_iv.shape, F32)
    for t in range(tap_tv.shape[1]):
        tapers += jnp.where(tap_iv[...] == t, tap_tv[:, t:t + 1], 0.0)
    lanes = lax.broadcasted_iota(jnp.int32, (tap_iv.shape[0], BLK), 1)
    coeff = jnp.zeros((tap_iv.shape[0], BLK), F32)
    for j in range(tap_iv.shape[1]):
        coeff += jnp.where(lists_v[:, j:j + 1] == lanes, tapers[:, j:j + 1], 0.0)
    c0[...] = coeff.astype(BF16)

    pl.semaphore_wait(
        barrier,
        (NS - 1) + (NZ - 1) + (NY - 1)
        + 4 - c_self.astype(jnp.int32)
        + NZ - home_diag.astype(jnp.int32),
    )

    sends = []

    def start(cp):
        cp.start()
        sends.append(cp)

    def core_copy(q, e):
        xx = mod(x + e, NX)
        return rc(core_send.at[q, xx], core_recv.at[q, xx], co_ss.at[q, e], co_rs.at[q, xx], partner)

    for q in range(2):
        for e in (2, 1, 3, 0):
            start(core_copy(q, e))

    pltpu.make_async_copy(a0.at[v], a1.at[v], a1_rs.at[v]).start()
    for j in range(PARTS):
        own = ens.at[:, pl.ds(pl.multiple_of(v * cells + j * width, width), width)]
        pltpu.make_async_copy(own, x1.at[j, v], x1_rs.at[j, v]).start()
    for d in range(1, NS):
        to = mod(v + d, NS)
        start(rc(a0.at[to], a1.at[v], a1_ss.at[d], a1_rs.at[v], dev(to, y, z)))

    def send_x1(j):
        for d in range(1, NS):
            to = mod(v + d, NS)
            src = ens.at[:, pl.ds(pl.multiple_of(to * cells + j * width, width), width)]
            start(rc(src, x1.at[j, v], x1_ss.at[j, d], x1_rs.at[j, v], dev(to, y, z)))

    @pl.when(home_diag)
    def _():
        pltpu.make_async_copy(var.at[v], vh, v_rs).start()
        for d in range(1, NS):
            to = mod(v + d, NS)
            rc(var.at[to], vh, v_ss.at[d], v_rs, dev(to, y, z)).start()

    for yy in range(NY):
        is_self = jnp.logical_and(c_self, y == yy)

        @pl.when(is_self)
        def _():
            pltpu.make_async_copy(c0, ch.at[c_row], c_rs.at[c_row]).start()

        @pl.when(jnp.logical_not(is_self))
        def _():
            rc(c0, ch.at[c_row], c_ss.at[yy], c_rs.at[c_row], dev(c_to, yy, v)).start()

    def sums(q):
        for e in (2, 1, 3, 0):
            xx = mod(x + e, NX)
            core_copy(q, e).wait_recv()

            def sum_one(g, carry):
                col = pl.multiple_of(g * (NS * data) + (NC * xx + c) * data + q * hdata, hdata)
                total = par_v[:, pl.ds(col, hdata)] + core_recv[q, xx, g].astype(F32)
                if e == 0:
                    own_sum[q, g] = total
                else:
                    rs_send[q, e - 1, g] = total.astype(BF16)
                return carry

            loop(NZ, sum_one, 2)
            if e:
                start(rc(rs_send.at[q, e - 1], rs_recv.at[q, e - 1], rs_ss.at[q, e - 1], rs_rs.at[q, e - 1], dev(NC * xx + c, y, z)))


    def forward_a(d):
        g = mod(z + d, NZ)
        arrived(a1.at[g], a1_rs.at[g])
        if d == 0:
            pltpu.make_async_copy(a1.at[g], a2.at[z], az_rs.at[z]).start()
        else:
            start(rc(a1.at[g], a2.at[z], az_ss.at[d], az_rs.at[z], dev(v, y, g)))

    def forward_x(j):
        for d in range(NZ):
            g = mod(z + d, NZ)
            arrived(x1.at[j, g], x1_rs.at[j, g])
            if d == 0:
                pltpu.make_async_copy(x1.at[j, g], x_all.at[j, y, z], xz_rs.at[j, z]).start()
            else:
                start(rc(x1.at[j, g], x_all.at[j, y, z], xz_ss.at[j, d], xz_rs.at[j, z], dev(v, y, g)))

    def predict(q):
        for e in range(1, NX):
            rc(rs_send.at[q, e - 1], rs_recv.at[q, e - 1], rs_ss.at[q, e - 1], rs_rs.at[q, e - 1], partner).wait_recv()

        def pred_one(g, carry):
            total = own_sum[q, g]
            for e in range(NX - 1):
                total += rs_recv[q, e, g].astype(F32)
            p1[q, g] = total.astype(BF16)
            return carry

        loop(NZ, pred_one, 2)
        pltpu.make_async_copy(p1.at[q, z], p_all.at[q, y, z], pz_rs.at[q, z]).start()
        for d in range(1, NZ):
            g = mod(z + d, NZ)
            start(rc(p1.at[q, g], p_all.at[q, y, z], pz_ss.at[q, d], pz_rs.at[q, z], dev(v, y, g)))

    def spread_p(q):
        for e in range(NZ):
            zs = mod(z + NZ - e, NZ)
            arrived(p_all.at[q, y, zs], pz_rs.at[q, zs])
        for d in (2, 1, 3):
            start(rc(p_all.at[q, y], p_all.at[q, y], py_ss.at[q, d], py_rs.at[q, y], dev(v, mod(y + d, NY), z)))

    ylo, yhi = mod(y + NY - 1, NY), mod(y + 1, NY)

    def spread_x(j):
        for e in range(NZ):
            zs = mod(z + NZ - e, NZ)
            arrived(x_all.at[j, y, zs], xz_rs.at[j, zs])
        for i, yy in enumerate((yhi, ylo)):
            start(rc(x_all.at[j, y], x_all.at[j, y], xy_ss.at[j, i], xy_rs.at[j, y], dev(v, yy, z)))

    def relay_x(j):
        for i, (src, to) in enumerate(((ylo, yhi), (yhi, ylo))):
            arrived(x_all.at[j, src], xy_rs.at[j, src])
            part = x_all.at[j, src, pl.ds(i * hz, hz)]
            start(rc(part, part, xr_ss.at[j, i], xr_rs.at[j, i], dev(v, to, z)))

    def settle_x(j):
        for i in range(2):
            arrived(x_all.at[j, mod(y + 2, NY), pl.ds(i * hz, hz)], xr_rs.at[j, i])

    def settle_a():
        for e in range(NZ):
            zs = mod(z + NZ - e, NZ)
            arrived(a2.at[zs], az_rs.at[zs])
        arrived(vh, v_rs)

    def weigh(q):
        def weight_one(o, carry):
            col = pl.ds(pl.multiple_of(o * BLK, BLK), BLK)
            acol = pl.ds(pl.multiple_of(q * hdata + o * BLK, BLK), BLK)
            innov = a2[:, :, acol].astype(F32) - p_all[q, y, :, :, col].astype(F32)
            w = innov.reshape(nl, BLK) / vh[pl.ds(q * nob + o, 1), :]
            wt[q * nob + o] = w.astype(BF16)
            return carry

        loop(nob, weight_one, 4)

    hl = nl // 4

    def moments(q):
        for d in range(1, NY):
            ys = mod(y + d, NY)
            arrived(p_all.at[q, ys], py_rs.at[q, ys])

        def moment_one(o, carry):
            col = pl.ds(pl.multiple_of(o * BLK, BLK), BLK)
            pred = p_all[q, :, :, :, col].astype(F32).reshape(nk, BLK).astype(BF16)
            mom = lax.dot_general(wt[q * nob + o], pred, (((1,), (1,)), ((), ())), preferred_element_type=F32)
            mom = mom - jnp.mean(mom, axis=1, keepdims=True)
            for h in range(2):
                m_f[h, pl.ds(o, nl, stride=nob), :] = mom[:, h * 128:(h + 1) * 128]
            return carry

        loop(nob, moment_one, 4)
        for k in range(2):
            def cast_m(i, carry):
                rows = pl.ds(pl.multiple_of((k * hl + i) * 2 * nob, 2 * nob), 2 * nob)
                for h in range(2):
                    m_all[q, k, v, i, :, h * 128:(h + 1) * 128] = m_f[h, rows, :].astype(BF16)
                return carry

            loop(hl, cast_m, 4)
            mine = m_all.at[q, k, v]
            for i, e in enumerate((1, 3)):
                start(rc(mine, mine, mx_ss.at[q, k, i], mx_rs.at[q, k, v], dev(mod(v + NC * e, NS), y, z)))
            start(rc(mine, mine, mc_ss.at[q, k, 0], mc_rs.at[q, k, v], partner))

    def relay_m(q, k):
        lo, hi = mod(v + NC * 3, NS), mod(v + NC, NS)
        for i, (src, to) in enumerate(((lo, hi), (hi, lo))):
            arrived(m_all.at[q, k, src], mx_rs.at[q, k, src])
            part = m_all.at[q, k, src, pl.ds(i * (hl // 2), hl // 2)]
            start(rc(part, part, mr_ss.at[q, k, i], mr_rs.at[q, k, i], dev(to, y, z)))
            whole = m_all.at[q, k, src]
            start(rc(whole, whole, mc_ss.at[q, k, 1 + i], mc_rs.at[q, k, src], partner))

    def finish_m(q, k):
        far = mod(v + NC * 2, NS)
        for i in range(2):
            arrived(m_all.at[q, k, far, pl.ds(i * (hl // 2), hl // 2)], mr_rs.at[q, k, i])
        whole = m_all.at[q, k, far]
        start(rc(whole, whole, mc_ss.at[q, k, 3], mc_rs.at[q, k, far], partner))

    def settle_m(q, k):
        for e in range(NX):
            vs = NC * mod(x + e, NX) + oc
            arrived(m_all.at[q, k, vs], mc_rs.at[q, k, vs])

    def spread_coeff():
        for j in range(4):
            arrived(ch.at[j], c_rs.at[j])
        rows = lax.broadcasted_iota(jnp.int32, (BLK, 2 * BLK), 0)
        cols = lax.broadcasted_iota(jnp.int32, (BLK, 2 * BLK), 1)
        block = lax.rem(cols // (2 * nob), NS) * (2 * nob) + (cols // BLK) * nob + lax.rem(cols, nob)
        tap = ch[...].reshape(nvb, BLK)
        res = []
        for parity in range(2):
            pick = jnp.logical_and(rows == block, lax.rem(cols // nob, 2) == parity)
            res.append(jnp.dot(tap, jnp.where(pick, 1.0, 0.0).astype(BF16), preferred_element_type=F32))
        return jnp.concatenate(res, axis=0).astype(BF16)

    def combine(coeff, k):
        def combine_one(i, carry):
            mom = m_all[:, k, :, i].reshape(2 * NS * 2 * nob, nk)
            com = jnp.dot(coeff, mom, preferred_element_type=F32)
            for parity in range(2):
                rows = pl.ds((k * hl + i) * 2 + parity, nvb, stride=nl)
                for h in range(2):
                    comb[h, rows, :] = com[parity * nvb:(parity + 1) * nvb, h * 128:(h + 1) * 128]
            return carry

        loop(hl, combine_one, 4)

    def centre(j):
        def centre_one(b, carry):
            col = pl.ds(pl.multiple_of(b * BLK, BLK), BLK)
            state = x_all[j, :, :, :, col].astype(F32).reshape(nk, BLK)
            xc[j * per_part + b] = (state - jnp.mean(state, axis=0, keepdims=True)).astype(BF16)
            return carry

        loop(per_part, centre_one, 4)

    def update(j):
        def update_one(b, carry):
            col = pl.ds(pl.multiple_of(b * BLK, BLK), BLK)
            rows = pl.ds(pl.multiple_of((j * per_part + b) * nl, nl), nl)
            left = jnp.concatenate([comb[h, rows, :].astype(BF16) for h in range(2)], axis=1)
            inc = jnp.dot(left, xc[j * per_part + b], preferred_element_type=F32)
            own = x_all[j, y, :, :, col].astype(F32)
            ost[j, :, :, col] = (own + inc.reshape(NZ, MEM, BLK) * (1.0 / (nk - 1))).astype(BF16)
            return carry

        loop(per_part, update_one, 4)
        dst = out.at[:, pl.ds(pl.multiple_of(v * cells + j * width, width), width)]
        for d in range(NZ):
            zt = mod(z + d, NZ)
            src = ost.at[j, zt]
            if d == 0:
                @pl.when(home_diag)
                def _():
                    pltpu.make_async_copy(src, dst, o_rs.at[j, v]).start()

                @pl.when(jnp.logical_not(home_diag))
                def _():
                    rc(src, dst, o_ss.at[j, 0], o_rs.at[j, v], dev(z, y, zt)).start()
            else:
                start(rc(src, dst, o_ss.at[j, d], o_rs.at[j, v], dev(z, y, zt)))

    sums(0)
    sums(1)
    send_x1(0)
    send_x1(1)
    send_x1(2)
    send_x1(3)
    for d in range(NZ):
        forward_a(d)
    predict(0)
    predict(1)
    spread_p(0)
    forward_x(0)
    spread_p(1)
    forward_x(1)
    settle_a()
    weigh(0)
    weigh(1)
    moments(0)
    spread_x(0)
    forward_x(2)
    moments(1)
    forward_x(3)
    spread_x(1)
    relay_x(0)
    relay_m(0, 0)
    relay_m(0, 1)
    finish_m(0, 0)
    finish_m(0, 1)
    settle_m(0, 0)
    spread_x(2)
    relay_x(1)
    relay_m(1, 0)
    relay_m(1, 1)
    finish_m(1, 0)
    finish_m(1, 1)
    coeff = spread_coeff()
    spread_x(3)
    relay_x(2)
    settle_m(1, 0)
    combine(coeff, 0)
    settle_m(0, 1)
    settle_m(1, 1)
    relay_x(3)
    combine(coeff, 1)
    settle_x(0)
    centre(0)
    update(0)
    settle_x(1)
    centre(1)
    update(1)
    settle_x(2)
    centre(2)
    update(2)
    settle_x(3)
    centre(3)
    update(3)

    for cp in sends:
        cp.wait_send()

    @pl.when(home_diag)
    def _():
        for d in range(1, NS):
            rc(var.at[0], vh, v_ss.at[d], v_rs, partner).wait_send()

    for yy in range(NY):
        @pl.when(jnp.logical_not(jnp.logical_and(c_self, y == yy)))
        def _():
            rc(c0, ch.at[c_row], c_ss.at[yy], c_rs.at[c_row], partner).wait_send()

    @pl.when(jnp.logical_not(home_diag))
    def _():
        for j in range(PARTS):
            rc(ost.at[j, 0], ost.at[j, 0], o_ss.at[j, 0], o_rs.at[j, v], partner).wait_send()

    for j in range(PARTS):
        for s in range(NS):
            arrived(out.at[:, pl.ds(s * cells + j * width, width)], o_rs.at[j, s])


def local(ensemble, partials, perturb, observed, variance, obs_lists, taper_index, taper_table):
    cells = ensemble.shape[1] // NS
    data = perturb.shape[1] // NS
    nob = data // BLK
    nl = NZ * MEM
    nvb = cells // BLK
    hdata = data // 2
    width = cells // PARTS
    dma = pltpu.SemaphoreType.DMA
    return pl.pallas_call(
        kernel,
        out_shape=jax.ShapeDtypeStruct(ensemble.shape, BF16),
        in_specs=[pl.BlockSpec(memory_space=pl.ANY)] * 8,
        out_specs=pl.BlockSpec(memory_space=pl.ANY),
        scratch_shapes=[
            pltpu.VMEM(partials.shape[1:], F32),
            pltpu.VMEM(perturb.shape, F32),
            pltpu.VMEM((1, observed.shape[0]), F32),
            pltpu.VMEM(obs_lists.shape, jnp.int32),
            pltpu.VMEM(taper_index.shape, jnp.int32),
            pltpu.VMEM((1, taper_table.shape[0]), F32),
            pltpu.VMEM((2, NX, NZ, MEM, hdata), BF16),
            pltpu.VMEM((2, NX, NZ, MEM, hdata), BF16),
            pltpu.VMEM((2, NX - 1, NZ, MEM, hdata), BF16),
            pltpu.VMEM((2, NX - 1, NZ, MEM, hdata), BF16),
            pltpu.VMEM((2, NZ, MEM, hdata), F32),
            pltpu.VMEM((NS, MEM, data), BF16),
            pltpu.VMEM((NS, MEM, data), BF16),
            pltpu.VMEM((NZ, MEM, data), BF16),
            pltpu.VMEM((nob, BLK), F32),
            pltpu.VMEM((16, BLK), BF16),
            pltpu.VMEM((4, 16, BLK), BF16),
            pltpu.VMEM((2, NZ, MEM, hdata), BF16),
            pltpu.VMEM((2, NY, NZ, MEM, hdata), BF16),
            pltpu.VMEM((PARTS, NS, MEM, width), BF16),
            pltpu.VMEM((PARTS, NY, NZ, MEM, width), BF16),
            pltpu.VMEM((nvb, NY * nl, BLK), BF16),
            pltpu.VMEM((nob, nl, BLK), BF16),
            pltpu.VMEM((2, nl * nob // 2, 128), F32),
            pltpu.VMEM((2, 2, NS, nl // 4, nob, NY * nl), BF16),
            pltpu.VMEM((2, nvb * nl, 128), F32),
            pltpu.VMEM((PARTS, NZ, MEM, width), BF16),
            dma((6,)),
            dma((2, NX)), dma((2, NX)),
            dma((2, NX - 1)), dma((2, NX - 1)),
            dma((PARTS, NS)), dma((PARTS, NS)),
            dma((NS,)), dma((NS,)),
            dma((NS,)), dma(()),
            dma((NY,)), dma((4,)),
            dma((PARTS, NZ)), dma((PARTS, NZ)),
            dma((NZ,)), dma((NZ,)),
            dma((2, NZ)), dma((2, NZ)),
            dma((2, NY)), dma((2, NY)),
            dma((PARTS, 2)), dma((PARTS, NY)),
            dma((PARTS, 2)), dma((PARTS, 2)),
            dma((2, 2, 2)), dma((2, 2, NS)),
            dma((2, 2, 2)), dma((2, 2, 2)),
            dma((2, 2, 4)), dma((2, 2, NS)),
            dma((PARTS, NZ)), dma((PARTS, NS)),
        ],
        compiler_params=pltpu.CompilerParams(
            collective_id=0, has_side_effects=True, vmem_limit_bytes=58 * 1024 * 1024
        ),
        cost_estimate=pl.CostEstimate(flops=900_000_000, bytes_accessed=8_000_000, transcendentals=0),
        name="update",
    )(
        ensemble,
        partials,
        perturb,
        observed.reshape(1, -1),
        variance.reshape(NS, nob, BLK),
        obs_lists,
        taper_index,
        taper_table.reshape(1, -1),
    )


def solution(mesh):
    return jax.shard_map(
        local,
        mesh=mesh,
        in_specs=(
            P("mem", "vox"),
            P("vox", "mem", None),
            P("mem", "vox"),
            P("vox"),
            P("vox"),
            P(("vox", "mem"), None),
            P(("vox", "mem"), None),
            P(),
        ),
        out_specs=P("mem", "vox"),
        check_vma=False,
    )
```
